32 devices in a mesh: expert: 8 (over z, y), hidden: 4 (over x, core).
Axes of the slice: x: 2, y: 2, z: 4, core: 2. Of those that a mesh axis runs over, the one named last changes fastest.
Arguments:
- tokens: bfloat16 [1024, 2048], P('expert', 'hidden'), may hold values from -6 to 6
- cotangent: bfloat16 [1024, 2048], P('expert', 'hidden'), may hold values from -6 to 6
- gate_weight: bfloat16 [16, 2048, 1408], P('expert', 'hidden'), may hold values from -0.125 to 0.125
- up_weight: bfloat16 [16, 2048, 1408], P('expert', 'hidden'), may hold values from -0.125 to 0.125
- down_weight: bfloat16 [16, 2048, 1408], P('expert', 'hidden'), may hold values from -0.15625 to 0.15625
- routing: int32 [1024, 6], P('expert'), may hold values from 0 to 15, all different within a row; in each aligned block of 128 rows (0 to 127, 128 to 255, ...) at most 64 rows name the same one
- route_weight: float32 [1024, 6], P('expert'), may hold values from 0.05 to 1
- merge_source: int32 [4], replicated, may hold values from 2 to 13, as said below
- merge_target: int32 [4], replicated, may hold values from 0 to 15, as said below
- neuron_perm: int32 [4, 1408], replicated, may hold values from 0 to 1407, as said below
Outputs:
- mixed: bfloat16 [1024, 2048], P('expert', 'hidden')
- grad_gate: bfloat16 [16, 2048, 1408], P('expert', 'hidden')
- grad_up: bfloat16 [16, 2048, 1408], P('expert', 'hidden')
- grad_down: bfloat16 [16, 2048, 1408], P('expert', 'hidden')
The draws below stay inside these ranges and needn't reach their ends.
Inputs may be any that keep to these rules, and one draw needn't show every extreme that they name: `routing`: in each aligned block of 128 tokens no expert is named more than 64 times, a bound that some block reaches. `merge_source`: 4 distinct experts, always including expert 2 and expert 16 - 3; merge_source and merge_target together hold exactly one expert of each aligned group of 2 consecutive expert numbers. `merge_target`: distinct experts, none of them a source, always including expert 0 and expert 16 - 1; see merge_source. `neuron_perm`: each row is a permutation of 0 to 1407.
All inputs are finite; a program needn't handle non-finite values.
Results may differ from the reference program's by a relative error of at most 0.019.
Values may be sent and summed in bfloat16 or wider, within the bound.
No kernel may reach another device: no remote copies, remote signals or barrier semaphores. Data moves between devices by JAX's collectives and lax.ppermute only.
A program may use at most 128 MiB of HBM per device.

```python
import math
import jax
import jax.numpy as jnp
import numpy as np
from jax import lax

D = 2048
FF = 1408
TOP = 6
EXP_DEV = 2
TOK_DEV = 128
EXPERTS = 16
TOKENS = 1024
MERGES = 4
MOST = 64
N_HIDDEN = 4


def pairing(key):
    holders = EXPERTS // EXP_DEV
    inner = (jax.random.permutation(jax.random.fold_in(key, 101), holders - 4) + 2).astype(jnp.int32)
    target_ends = jnp.array([0, holders - 1], dtype=jnp.int32)
    source_ends = jnp.array([1, holders - 2], dtype=jnp.int32)
    target_dev = jnp.concatenate([target_ends, inner[:MERGES - 2]])
    source_dev = jnp.concatenate([source_ends, inner[MERGES - 2:]])
    target_places = jax.random.randint(jax.random.fold_in(key, 202), (MERGES,), 0, EXP_DEV).astype(jnp.int32)
    target_places = target_places.at[0].set(0).at[1].set(EXP_DEV - 1)
    source_places = jax.random.randint(jax.random.fold_in(key, 404), (MERGES,), 0, EXP_DEV).astype(jnp.int32)
    source_places = source_places.at[0].set(0).at[1].set(EXP_DEV - 1)
    return ((source_dev * EXP_DEV + source_places).astype(jnp.int32), (target_dev * EXP_DEV + target_places).astype(jnp.int32))


def draw_merge_source(key, part):
    return pairing(key)[0]


def draw_merge_target(key, part):
    return pairing(key)[1]


def draw_neuron_perm(key, part):
    streams = jax.random.split(jax.random.fold_in(key, 303), MERGES)
    return jax.vmap(lambda stream: jax.random.permutation(stream, FF))(streams).astype(jnp.int32)


def steps_of(key, extent, cuts, least, largest):
    gain, own = 1.0, jax.random.fold_in(key, 6)
    for position, parts in cuts:
        draws = jnp.exp(jax.random.uniform(jax.random.fold_in(own, position), (parts,), jnp.float32, least / len(cuts), largest / len(cuts)))
        gain = gain * jnp.repeat(draws, extent[position] // parts).reshape([-1 if axis == position else 1 for axis in range(len(extent))])
    return gain


def deal_out(key, own, number, rows, amount, top, bound, skew):
    order = jax.random.permutation(key, amount)
    crowded, common = shares(amount, rows * top, bound, skew, True), shares(amount, rows * top, bound, skew, False)
    places = jnp.arange(amount)

    def named(tallies, turn):
        used = int((tallies > 0).sum())
        fixed = max(1, used // 4)
        passed = fixed + (places - fixed + turn * (used - fixed)) % max(1, amount - fixed)
        return jnp.zeros((amount,), jnp.int32).at[order[jnp.where(places < fixed, places, passed)]].set(jnp.asarray(tallies, jnp.int32))

    tallies = jnp.where(number % 4 == 0, named(crowded, number // 4), named(common, number - number // 4 - 1))
    mixed = jax.random.permutation(jax.random.fold_in(own, 3), amount)
    source_of, receiver = mixed[0:amount // 2 * 2:2], mixed[1:amount // 2 * 2:2]
    margin = jnp.minimum(tallies[source_of] - 1, bound - tallies[receiver]) // 2
    margin = jnp.where((source_of == order[0]) | (receiver == order[0]) | (tallies[receiver] == 0), 0, jnp.maximum(margin, 0))
    passed = jax.random.randint(jax.random.fold_in(own, 4), (amount // 2,), 0, 1 << 20) % (margin + 1)
    tallies = tallies.at[source_of].add(-passed).at[receiver].add(passed)
    members = jnp.searchsorted(jnp.cumsum(tallies), jnp.arange(rows * top), side="right").astype(jnp.int32)
    listing = members.reshape(top, rows).T
    listing = listing[jax.random.permutation(jax.random.fold_in(own, 1), rows)]
    turn = jax.random.randint(jax.random.fold_in(own, 2), (rows, 1), 0, top)
    return jnp.take_along_axis(listing, (jnp.arange(top)[None, :] + turn) % top, axis=1)


def shares(count, total, limit, skew, full):
    weights = [(1 << 20) // math.isqrt(grade ** skew) + 1 for grade in range(1, count + 1)]
    largest = limit if full else min(limit, max(-(-total // count), total * weights[0] // sum(weights)))
    least = 1 if total - largest >= count - 1 else 0
    given, rest = [largest] + [least] * (count - 1), total - largest - least * (count - 1)
    while rest > 0:
        candidates = [i for i in range(1, count) if given[i] < largest] or [i for i in range(1, count) if given[i] < limit]
        pool, remaining = sum([weights[i] for i in candidates]), rest
        for i in candidates:
            more = min(limit - given[i], max(1, remaining * weights[i] // pool), rest)
            given[i] = given[i] + more
            rest = rest - more
    return np.array(given)


def noise(own_key, shape, width, limit, shards=(), held_as=jnp.bfloat16):
    entries = jax.random.normal(own_key, shape, jnp.float32) * width
    if len(shards) > 0:
        entries = steps_of(own_key, shape, shards, -0.22, 0.18) * entries
    return jnp.clip(entries, min=-limit, max=limit).astype(held_as)


def setup_inputs(seed: int = 0) -> dict:
    streams_of = jax.random.split(jax.random.key(seed), 11)
    tokens = noise(streams_of[0], (TOKENS, D), 1.0, 6.0, ((0, 8), (1, 4)))
    cotangent = noise(streams_of[1], (TOKENS, D), 1.0, 6.0, ((0, 8), (1, 4)))
    gate_weight = noise(streams_of[2], (EXPERTS, D, FF), D ** -0.5, 0.125, ((0, 8), (1, 4)))
    up_weight = noise(streams_of[3], (EXPERTS, D, FF), D ** -0.5, 0.125, ((0, 8), (1, 4)))
    down_weight = noise(streams_of[4], (EXPERTS, D, FF), FF ** -0.5, 0.15625, ((0, 8), (1, 4)))
    routing_keys = jax.random.split(jax.random.fold_in(streams_of[5], 1), TOKENS // TOK_DEV)
    routing_turns = jax.random.permutation(jax.random.fold_in(streams_of[5], 3), TOKENS // TOK_DEV)
    routing = jax.vmap(lambda own, number: deal_out(jax.random.fold_in(streams_of[5], 2), own, number, TOK_DEV, EXPERTS, TOP, MOST, 2))(routing_keys, routing_turns).reshape((TOKENS, TOP))
    route_weight = jnp.clip(0.05 + 0.95 * jax.random.uniform(streams_of[6], (TOKENS, TOP), jnp.float32) ** steps_of(streams_of[6], (TOKENS, TOP), ((0, 8),), -0.2, 0.2), 0.05, 1.0)
    merge_source = draw_merge_source(jax.random.fold_in(streams_of[10], 71), 0)
    merge_target = draw_merge_target(jax.random.fold_in(streams_of[10], 71), 0)
    neuron_perm = draw_neuron_perm(jax.random.fold_in(streams_of[10], 71), 0)
    return dict(tokens=tokens, cotangent=cotangent, gate_weight=gate_weight, up_weight=up_weight, down_weight=down_weight, routing=routing, route_weight=route_weight, merge_source=merge_source, merge_target=merge_target, neuron_perm=neuron_perm)


def silu_parts(values):
    sigma = jax.nn.sigmoid(values)
    return values * sigma, sigma * (1.0 + values * (1.0 - sigma))


def shard_sums(activ, weight, group_n, row_count):
    left = activ.astype(jnp.float32).reshape(group_n, row_count, N_HIDDEN, D // N_HIDDEN)
    right = weight.astype(jnp.float32).reshape(group_n, N_HIDDEN, D // N_HIDDEN, FF)
    pieces = jnp.einsum('grhd,ghdf->ghrf', left, right)
    pieces = lax.optimization_barrier(pieces.astype(jnp.bfloat16))
    return jnp.sum(pieces.astype(jnp.float32), axis=1)


def merge_weight(weight, merge_source, merge_target, neuron_perm):
    moved = jax.vmap(lambda block, order: block[:, order])(weight[merge_source], neuron_perm)
    blended = (0.5 * (weight[merge_target].astype(jnp.float32) + moved.astype(jnp.float32))).astype(jnp.bfloat16)
    return weight.at[merge_target].set(blended)


def reference(tokens, cotangent, gate_weight, up_weight, down_weight, routing, route_weight, merge_source, merge_target, neuron_perm):
    devices_n = EXPERTS // EXP_DEV
    groups = EXP_DEV + 1
    row_count = devices_n * MOST
    slot_total = devices_n * groups * row_count
    assign_n = TOKENS * TOP
    expert_ids = jnp.arange(EXPERTS, dtype=jnp.int32)
    source_hit = merge_source[:, None] == expert_ids[None, :]
    is_source = jnp.any(source_hit, axis=0)
    mapped = jnp.where(is_source, jnp.sum(jnp.where(source_hit, merge_target[:, None], 0), axis=0), expert_ids).astype(jnp.int32)
    group_of = jnp.where(is_source, EXP_DEV, mapped % EXP_DEV).astype(jnp.int32)
    flat_ids = routing.reshape(-1).astype(jnp.int32)
    expert_hot = (flat_ids[:, None] == expert_ids[None, :]).astype(jnp.int32).reshape(devices_n, TOK_DEV * TOP, EXPERTS)
    rank_in = (jnp.sum(jnp.cumsum(expert_hot, axis=1) * expert_hot, axis=2) - 1).reshape(-1).astype(jnp.int32)
    block_of = (jnp.arange(assign_n, dtype=jnp.int32) // (TOK_DEV * TOP)).astype(jnp.int32)
    slot_index = ((mapped[flat_ids] // EXP_DEV) * (groups * row_count) + group_of[flat_ids] * row_count + block_of * MOST + rank_in).astype(jnp.int32)
    token_of = (jnp.arange(assign_n, dtype=jnp.int32) // TOP).astype(jnp.int32)
    weight_flat = route_weight.reshape(-1)
    slot_x = jnp.zeros((slot_total, D), jnp.bfloat16).at[slot_index].set(tokens[token_of])
    scaled = (weight_flat[:, None] * cotangent[token_of].astype(jnp.float32)).astype(jnp.bfloat16)
    slot_dy = jnp.zeros((slot_total, D), jnp.bfloat16).at[slot_index].set(scaled)

    merged_gate = merge_weight(gate_weight, merge_source, merge_target, neuron_perm).reshape(devices_n, EXP_DEV, D, FF)
    merged_up = merge_weight(up_weight, merge_source, merge_target, neuron_perm).reshape(devices_n, EXP_DEV, D, FF)
    merged_down = merge_weight(down_weight, merge_source, merge_target, neuron_perm).reshape(devices_n, EXP_DEV, D, FF)
    target_dev = merge_target // EXP_DEV
    pair_hit = target_dev[:, None] == jnp.arange(devices_n, dtype=jnp.int32)[None, :]
    target_slot = jnp.sum(jnp.where(pair_hit, (merge_target % EXP_DEV)[:, None], 0), axis=0).astype(jnp.int32)

    def per_device(packed):
        w_gate, w_up, w_down, slot_k, inputs_x, inputs_dy = packed

        def widen(weight):
            chosen = lax.dynamic_index_in_dim(weight, slot_k, 0, keepdims=True)
            return jnp.concatenate([weight, chosen], axis=0)

        w_gate, w_up, w_down = widen(w_gate), widen(w_up), widen(w_down)
        gate_sum = shard_sums(inputs_x, w_gate, groups, row_count)
        up_sum = shard_sums(inputs_x, w_up, groups, row_count)
        active, slope = silu_parts(gate_sum)
        hidden_act = (active * up_sum).astype(jnp.bfloat16)
        outputs_y = jnp.einsum('grf,gdf->grd', hidden_act.astype(jnp.float32), w_down.astype(jnp.float32)).astype(jnp.bfloat16)
        grad_down = jnp.einsum('grd,grf->gdf', inputs_dy.astype(jnp.float32), hidden_act.astype(jnp.float32))
        back_sum = shard_sums(inputs_dy, w_down, groups, row_count)
        grad_gate_act = (back_sum * up_sum * slope).astype(jnp.bfloat16)
        grad_up_act = (back_sum * active).astype(jnp.bfloat16)
        grad_gate = jnp.einsum('grd,grf->gdf', inputs_x.astype(jnp.float32), grad_gate_act.astype(jnp.float32))
        grad_up = jnp.einsum('grd,grf->gdf', inputs_x.astype(jnp.float32), grad_up_act.astype(jnp.float32))

        def fold(grad):
            base = grad[:EXP_DEV]
            extra = lax.dynamic_index_in_dim(base, slot_k, 0, keepdims=False) + grad[EXP_DEV]
            return lax.dynamic_update_index_in_dim(base, extra, slot_k, 0).astype(jnp.bfloat16)

        return outputs_y, fold(grad_gate), fold(grad_up), fold(grad_down)

    packed = (merged_gate, merged_up, merged_down, target_slot,
              slot_x.reshape(devices_n, groups, row_count, D), slot_dy.reshape(devices_n, groups, row_count, D))
    outputs_y, grad_gate, grad_up, grad_down = lax.map(per_device, packed)
    gathered = outputs_y.reshape(slot_total, D)[slot_index].astype(jnp.float32) * weight_flat[:, None]
    mixed = jnp.sum(gathered.reshape(TOKENS, TOP, D), axis=1).astype(jnp.bfloat16)
    return (mixed, grad_gate.reshape(EXPERTS, D, FF), grad_up.reshape(EXPERTS, D, FF), grad_down.reshape(EXPERTS, D, FF))
```

```python
import functools

import jax
import jax.numpy as jnp
from jax import lax
from jax.sharding import PartitionSpec as P

F32 = jnp.float32
INLINE = 8
BF16 = jnp.bfloat16


def dot(a, b, ca, cb):
    return lax.dot_general(a, b, (((ca,), (cb,)), ((), ())), preferred_element_type=F32)


def xor_pairs(count, bits):
    return [(i, i ^ bits) for i in range(count)]


def with_partner(count, apart, run, *args):
    def exchange(bits, values):
        return [lax.ppermute(v, "expert", xor_pairs(count, bits)) for v in values]

    choices = range(1, count)
    if count <= INLINE:
        branches = [functools.partial(run, functools.partial(exchange, b)) for b in choices]
        return lax.switch(apart - 1, branches, *args)
    branches = [functools.partial(exchange, b) for b in choices]
    return run(lambda values: lax.switch(apart - 1, branches, values), *args)


def activations(gate_sum, up_sum, back_sum):
    sigma = jax.nn.sigmoid(gate_sum)
    active = gate_sum * sigma
    slope = sigma * (1.0 + gate_sum * (1.0 - sigma))
    return (
        (active * up_sum).astype(BF16),
        (back_sum * up_sum * slope).astype(BF16),
        (back_sum * active).astype(BF16),
    )


def shards(
    tokens,
    cotangent,
    gate_weight,
    up_weight,
    down_weight,
    routing,
    route_weight,
    merge_source,
    merge_target,
    neuron_perm,
):
    devices_n = lax.axis_size("expert")
    hidden_n = lax.axis_size("hidden")
    me = lax.axis_index("expert")
    low_bit = lax.axis_index("hidden") % 2
    exp_local, width, neurons = gate_weight.shape
    experts = exp_local * devices_n
    tok_local, top_count = routing.shape
    tok_all = tok_local * devices_n
    depth = max(2, tok_local * top_count * 4 // (3 * experts))
    slots = devices_n * depth
    half = neurons // 2
    weights = (gate_weight, up_weight, down_weight)

    source_dev = merge_source // exp_local
    target_dev = merge_target // exp_local
    is_source = source_dev == me
    is_target = target_dev == me
    mine = is_source | is_target
    am_target = jnp.any(is_target)
    partner = jnp.sum(jnp.where(is_source, target_dev, 0) + jnp.where(is_target, source_dev, 0))
    source_e = jnp.sum(jnp.where(mine, merge_source, 0))
    target_e = jnp.sum(jnp.where(mine, merge_target, 0))
    merged_slot = jnp.where(am_target, target_e, source_e) % exp_local
    other_slot = exp_local - 1 - merged_slot
    other_e = me * exp_local + other_slot
    perm = jnp.sum(jnp.where(mine[:, None], neuron_perm, 0), axis=0)

    expert_ids = jnp.arange(experts, dtype=jnp.int32)
    route = jnp.sum(
        jnp.where(routing[:, :, None] == expert_ids, route_weight[:, :, None], 0.0), axis=1
    )
    high = lax.reduce_precision(route, 8, 7)
    middle = lax.reduce_precision(route - high, 8, 7)
    low = route - high - middle
    pieces = jnp.concatenate([high, middle, low], axis=1).astype(BF16)
    pad = -pieces.shape[1] % 128
    payload = jnp.concatenate(
        [tokens, cotangent, jnp.pad(pieces, ((0, 0), (0, pad)))], axis=1
    )
    gathered = lax.all_gather(payload, "expert", axis=0, tiled=True)

    order = jnp.where(am_target, jnp.arange(neurons, dtype=jnp.int32), perm)
    keep_order = jnp.where(am_target, order[:half], order[half:])
    send_order = jnp.where(am_target, order[half:], order[:half])
    columns = jnp.arange(neurons, dtype=jnp.int32)
    keep_hot = (keep_order[:, None] == columns[None, :]).astype(BF16)
    send_hot = (send_order[:, None] == columns[None, :]).astype(BF16)
    chosen = [lax.dynamic_index_in_dim(w, merged_slot, 0, keepdims=False) for w in weights]
    others = [lax.dynamic_index_in_dim(w, other_slot, 0, keepdims=False) for w in weights]
    sends = [dot(send_hot, w, 1, 1).astype(BF16) for w in chosen]
    keeps = [dot(keep_hot, w, 1, 1).astype(BF16) for w in chosen]

    inputs_x = gathered[:, :width]
    inputs_c = gathered[:, width : 2 * width]
    parts = gathered[:, 2 * width : 2 * width + 3 * experts].astype(F32)
    route_all = parts[:, :experts] + parts[:, experts : 2 * experts] + parts[:, 2 * experts :]
    merged_hit = (expert_ids == source_e) | (expert_ids == target_e)
    merged_p = jnp.sum(jnp.where(merged_hit, route_all, 0.0), axis=1)
    other_p = jnp.sum(jnp.where(expert_ids == other_e, route_all, 0.0), axis=1)
    merged_dy = (merged_p[:, None] * inputs_c.astype(F32)).astype(BF16)

    named = (other_p > 0.0).reshape(devices_n, tok_local)
    upper = jnp.arange(tok_local)[:, None] <= jnp.arange(tok_local)[None, :]
    rank = dot(named.astype(BF16), upper.astype(BF16), 1, 0).astype(jnp.int32) - 1
    block = (jnp.arange(devices_n, dtype=jnp.int32) + (1 - low_bit) * (devices_n // 2)) % devices_n
    place = jnp.where(named, block[:, None] * depth + rank, -1).reshape(tok_all)
    slot_hot = jnp.arange(slots, dtype=jnp.int32)[:, None] == place[None, :]
    slot_p = jnp.sum(jnp.where(slot_hot, other_p[None, :], 0.0), axis=1)
    slot_hot = slot_hot.astype(BF16)
    other_x = dot(slot_hot, inputs_x, 1, 0).astype(BF16)
    other_dy = (dot(slot_hot, inputs_c, 1, 0) * slot_p[:, None]).astype(BF16)

    def reduced(send_part, keep_part):
        total = keep_part
        if hidden_n > 1:
            total = total + lax.ppermute(send_part.astype(BF16), "hidden", xor_pairs(hidden_n, 1))
        bit = 2
        while bit < hidden_n:
            rounded = total.astype(BF16)
            total = rounded.astype(F32) + lax.ppermute(
                rounded, "hidden", xor_pairs(hidden_n, bit)
            ).astype(F32)
            bit *= 2
        return total

    def swapped(value):
        return lax.ppermute(value, "hidden", xor_pairs(hidden_n, 1))

    slots_half = slots // 2
    quarter = half // 2

    def forward(
        exchange, sends, keeps, others, inputs_x, merged_dy, other_x, other_dy, slot_p, merged_p
    ):
        arrived = exchange(sends)
        sums = [
            reduced(dot(value[:slots_half], w, 1, 0), dot(value[slots_half:], w, 1, 0))
            for value, w in zip((other_x, other_x, other_dy), others)
        ]
        acts = activations(*sums)
        other_acts = [jnp.concatenate([swapped(a), a], axis=0) for a in acts]
        other_y = dot(other_acts[0], others[2], 1, 1)
        other_y = (other_y * slot_p[:, None]).astype(BF16)

        merged = [
            (0.5 * (k.astype(F32) + a.astype(F32))).astype(BF16)
            for k, a in zip(keeps, arrived)
        ]
        sums = []
        for value, w in zip((inputs_x, inputs_x, merged_dy), merged):
            w_send = lax.dynamic_slice_in_dim(w, (1 - low_bit) * quarter, quarter, 0)
            w_keep = lax.dynamic_slice_in_dim(w, low_bit * quarter, quarter, 0)
            sums.append(reduced(dot(w_send, value, 1, 1), dot(w_keep, value, 1, 1)))
        acts = activations(*sums)
        merged_acts = []
        for a in acts:
            b = swapped(a)
            merged_acts.append(
                jnp.concatenate(
                    [jnp.where(low_bit == 0, a, b), jnp.where(low_bit == 0, b, a)], axis=0
                )
            )
        merged_y = dot(merged_acts[0], merged[2], 0, 0)
        mixed = dot(slot_hot, other_y, 0, 0) + merged_p[:, None] * merged_y
        return mixed.astype(BF16), other_acts, merged_acts

    mixed, other_acts, merged_acts = with_partner(
        devices_n,
        me ^ partner,
        forward,
        sends,
        keeps,
        others,
        inputs_x,
        merged_dy,
        other_x,
        other_dy,
        slot_p,
        merged_p,
    )
    mixed = lax.psum_scatter(mixed, "expert", scatter_dimension=0, tiled=True)

    def backward(exchange, inputs_x, merged_dy, merged_acts):
        h, dg, du = merged_acts
        own = [
            dot(value, a, 0, 1).astype(BF16)
            for value, a in ((merged_dy, h), (inputs_x, dg), (inputs_x, du))
        ]
        return own, exchange(own)

    own, returned = with_partner(
        devices_n, me ^ partner, backward, inputs_x, merged_dy, merged_acts
    )
    h, dg, du = other_acts
    outs = []
    for value, a, mine_half, far_half in zip(
        (other_dy, other_x, other_x), (h, dg, du), own, returned
    ):
        other_grad = dot(value, a, 0, 0).astype(BF16)
        merged_grad = jnp.where(
            am_target, jnp.concatenate([mine_half, far_half], axis=1), jnp.zeros((), BF16)
        )
        outs.append(
            jnp.where(
                merged_slot == 0,
                jnp.stack([merged_grad, other_grad]),
                jnp.stack([other_grad, merged_grad]),
            )
        )
    grad_down, grad_gate, grad_up = outs
    return mixed, grad_gate, grad_up, grad_down


def solution(mesh):
    placed = (
        P("expert", "hidden"),
        P("expert", "hidden"),
        P("expert", "hidden", None),
        P("expert", "hidden", None),
        P("expert", "hidden", None),
        P("expert", None),
        P("expert", None),
        P(),
        P(),
        P(),
    )
    return jax.shard_map(
        shards,
        mesh=mesh,
        in_specs=placed,
        out_specs=(
            P("expert", "hidden"),
            P("expert", "hidden", None),
            P("expert", "hidden", None),
            P("expert", "hidden", None),
        ),
        check_vma=False,
    )
```

```python
import functools

import jax
import jax.numpy as jnp
from jax import lax
from jax.sharding import PartitionSpec as P

F32 = jnp.float32
BF16 = jnp.bfloat16


def dot(a, b, ca, cb):
    return lax.dot_general(a, b, (((ca,), (cb,)), ((), ())), preferred_element_type=F32)


def xor_pairs(count, bits):
    return [(i, i ^ bits) for i in range(count)]


def with_partner(count, apart, value):
    branches = [
        functools.partial(lax.ppermute, axis_name="expert", perm=xor_pairs(count, bits))
        for bits in range(1, count)
    ]
    return lax.switch(apart - 1, branches, value)


def ring_gather(value, count, me):
    rows = value.shape[0]
    ring = [(i, (i + 2) % count) for i in range(count)]
    result = jnp.zeros((rows * count, value.shape[1]), value.dtype)
    for step in range(count // 2):
        if step > 0:
            value = lax.ppermute(value, "expert", ring)
        twin = lax.ppermute(value, "expert", xor_pairs(count, 1))
        for block, owner in ((value, me), (twin, me ^ 1)):
            at = (owner - 2 * step) % count * rows
            result = lax.dynamic_update_slice_in_dim(result, block, at, 0)
    return result


def ring_scatter(partial, count, me):
    rows = partial.shape[0] // count
    ring = [(i, (i + 2) % count) for i in range(count)]

    def block(owner):
        return lax.dynamic_slice_in_dim(partial, owner % count * rows, rows, 0)

    total = None
    for step in range(count // 2):
        twin = lax.ppermute(
            block((me ^ 1) - 2 * (step + 1)).astype(BF16), "expert", xor_pairs(count, 1)
        )
        own = block(me - 2 * (step + 1)).astype(F32) + twin.astype(F32)
        if step > 0:
            own = own + lax.ppermute(total, "expert", ring).astype(F32)
        total = own.astype(BF16)
    return total


def activations(gate_sum, up_sum, back_sum):
    sigma = jax.nn.sigmoid(gate_sum)
    active = gate_sum * sigma
    slope = sigma * (1.0 + gate_sum * (1.0 - sigma))
    return (
        (active * up_sum).astype(BF16),
        (back_sum * up_sum * slope).astype(BF16),
        (back_sum * active).astype(BF16),
    )


def shards(
    tokens,
    cotangent,
    gate_weight,
    up_weight,
    down_weight,
    routing,
    route_weight,
    merge_source,
    merge_target,
    neuron_perm,
):
    devices_n = lax.axis_size("expert")
    hidden_n = lax.axis_size("hidden")
    me = lax.axis_index("expert")
    low_bit = lax.axis_index("hidden") % 2
    exp_local, width, neurons = gate_weight.shape
    experts = exp_local * devices_n
    tok_local, top_count = routing.shape
    tok_all = tok_local * devices_n
    depth = max(2, tok_local * top_count * 4 // (3 * experts))
    slots = devices_n * depth
    half = neurons // 2
    weights = (gate_weight, up_weight, down_weight)

    source_dev = merge_source // exp_local
    target_dev = merge_target // exp_local
    is_source = source_dev == me
    is_target = target_dev == me
    mine = is_source | is_target
    am_target = jnp.any(is_target)
    partner = jnp.sum(jnp.where(is_source, target_dev, 0) + jnp.where(is_target, source_dev, 0))
    source_e = jnp.sum(jnp.where(mine, merge_source, 0))
    target_e = jnp.sum(jnp.where(mine, merge_target, 0))
    merged_slot = jnp.where(am_target, target_e, source_e) % exp_local
    other_slot = exp_local - 1 - merged_slot
    other_e = me * exp_local + other_slot
    perm = jnp.sum(jnp.where(mine[:, None], neuron_perm, 0), axis=0)

    expert_ids = jnp.arange(experts, dtype=jnp.int32)
    route = jnp.sum(
        jnp.where(routing[:, :, None] == expert_ids, route_weight[:, :, None], 0.0), axis=1
    )
    high = lax.reduce_precision(route, 8, 7)
    middle = lax.reduce_precision(route - high, 8, 7)
    low = route - high - middle
    pieces = jnp.concatenate([high, middle, low], axis=1).astype(BF16)
    pad = -pieces.shape[1] % 128
    payload = jnp.concatenate([tokens, jnp.pad(pieces, ((0, 0), (0, pad)))], axis=1)
    gathered = ring_gather(payload, devices_n, me)
    inputs_c = ring_gather(cotangent, devices_n, me)

    order = jnp.where(am_target, jnp.arange(neurons, dtype=jnp.int32), perm)
    keep_order = jnp.where(am_target, order[:half], order[half:])
    send_order = jnp.where(am_target, order[half:], order[:half])
    columns = jnp.arange(neurons, dtype=jnp.int32)
    keep_hot = (keep_order[:, None] == columns[None, :]).astype(BF16)
    send_hot = (send_order[:, None] == columns[None, :]).astype(BF16)
    chosen = [lax.dynamic_index_in_dim(w, merged_slot, 0, keepdims=False) for w in weights]
    others = [lax.dynamic_index_in_dim(w, other_slot, 0, keepdims=False) for w in weights]
    sends = [dot(send_hot, w, 1, 1).astype(BF16) for w in chosen]
    keeps = [dot(keep_hot, w, 1, 1).astype(BF16) for w in chosen]

    inputs_x = gathered[:, :width]
    parts = gathered[:, width : width + 3 * experts].astype(F32)
    route_all = parts[:, :experts] + parts[:, experts : 2 * experts] + parts[:, 2 * experts :]
    merged_hit = (expert_ids == source_e) | (expert_ids == target_e)
    merged_p = jnp.sum(jnp.where(merged_hit, route_all, 0.0), axis=1)
    other_p = jnp.sum(jnp.where(expert_ids == other_e, route_all, 0.0), axis=1)
    merged_dy = (merged_p[:, None] * inputs_c.astype(F32)).astype(BF16)

    named = (other_p > 0.0).reshape(devices_n, tok_local)
    upper = jnp.arange(tok_local)[:, None] <= jnp.arange(tok_local)[None, :]
    rank = dot(named.astype(BF16), upper.astype(BF16), 1, 0).astype(jnp.int32) - 1
    block = (jnp.arange(devices_n, dtype=jnp.int32) + (1 - low_bit) * (devices_n // 2)) % devices_n
    place = jnp.where(named, block[:, None] * depth + rank, -1).reshape(tok_all)
    slot_hot = jnp.arange(slots, dtype=jnp.int32)[:, None] == place[None, :]
    slot_p = jnp.sum(jnp.where(slot_hot, other_p[None, :], 0.0), axis=1)
    slot_hot = slot_hot.astype(BF16)
    other_x = dot(slot_hot, inputs_x, 1, 0).astype(BF16)
    other_dy = (dot(slot_hot, inputs_c, 1, 0) * slot_p[:, None]).astype(BF16)

    def reduced(send_part, keep_part):
        total = keep_part
        if hidden_n > 1:
            total = total + lax.ppermute(send_part.astype(BF16), "hidden", xor_pairs(hidden_n, 1))
        bit = 2
        while bit < hidden_n:
            rounded = total.astype(BF16)
            total = rounded.astype(F32) + lax.ppermute(
                rounded, "hidden", xor_pairs(hidden_n, bit)
            ).astype(F32)
            bit *= 2
        return total

    def swapped(value):
        return lax.ppermute(value, "hidden", xor_pairs(hidden_n, 1))

    slots_half = slots // 2
    quarter = half // 2

    apart = me ^ partner
    arrived = [with_partner(devices_n, apart, value) for value in sends]

    sums = [
        reduced(dot(value[:slots_half], w, 1, 0), dot(value[slots_half:], w, 1, 0))
        for value, w in zip((other_x, other_x, other_dy), others)
    ]
    other_h, other_dg, other_du = [
        jnp.concatenate([swapped(a), a], axis=0) for a in activations(*sums)
    ]
    other_y = (dot(other_h, others[2], 1, 1) * slot_p[:, None]).astype(BF16)
    other_grads = [
        dot(value, a, 0, 0).astype(BF16)
        for value, a in ((other_x, other_dg), (other_x, other_du), (other_dy, other_h))
    ]

    merged = [
        (0.5 * (k.astype(F32) + a.astype(F32))).astype(BF16) for k, a in zip(keeps, arrived)
    ]
    sums = []
    for value, w in zip((inputs_x, inputs_x, merged_dy), merged):
        w_send = lax.dynamic_slice_in_dim(w, (1 - low_bit) * quarter, quarter, 0)
        w_keep = lax.dynamic_slice_in_dim(w, low_bit * quarter, quarter, 0)
        sums.append(reduced(dot(w_send, value, 1, 1), dot(w_keep, value, 1, 1)))
    merged_acts = []
    for a in activations(*sums):
        b = swapped(a)
        merged_acts.append(
            jnp.concatenate(
                [jnp.where(low_bit == 0, a, b), jnp.where(low_bit == 0, b, a)], axis=0
            )
        )
    merged_h, merged_dg, merged_du = merged_acts
    merged_y = dot(merged_h, merged[2], 0, 0)
    mixed = dot(slot_hot, other_y, 0, 0) + merged_p[:, None] * merged_y
    mixed = ring_scatter(mixed.astype(BF16), devices_n, me)

    down_half = dot(merged_dy, merged_h, 0, 1).astype(BF16)
    gate_half = dot(inputs_x, merged_dg, 0, 1).astype(BF16)
    up_half = dot(inputs_x, merged_du, 0, 1).astype(BF16)
    far_down = with_partner(devices_n, apart, down_half)
    far_gate = with_partner(devices_n, apart, gate_half)
    far_up = with_partner(devices_n, apart, up_half)

    outs = []
    for other_grad, own_half, far_half in zip(
        other_grads, (gate_half, up_half, down_half), (far_gate, far_up, far_down)
    ):
        merged_grad = jnp.where(
            am_target, jnp.concatenate([own_half, far_half], axis=1), jnp.zeros((), BF16)
        )
        out = jnp.zeros((exp_local, width, neurons), BF16)
        out = lax.dynamic_update_slice_in_dim(out, other_grad[None], other_slot, 0)
        outs.append(lax.dynamic_update_slice_in_dim(out, merged_grad[None], merged_slot, 0))
    return (mixed, *outs)


def solution(mesh):
    placed = (
        P("expert", "hidden"),
        P("expert", "hidden"),
        P("expert", "hidden", None),
        P("expert", "hidden", None),
        P("expert", "hidden", None),
        P("expert", None),
        P("expert", None),
        P(),
        P(),
        P(),
    )
    return jax.shard_map(
        shards,
        mesh=mesh,
        in_specs=placed,
        out_specs=(
            P("expert", "hidden"),
            P("expert", "hidden", None),
            P("expert", "hidden", None),
            P("expert", "hidden", None),
        ),
        check_vma=False,
    )
```

```python
import functools

import jax
import jax.numpy as jnp
from jax import lax
from jax.experimental import pallas as pl
from jax.experimental.pallas import tpu as pltpu
from jax.sharding import PartitionSpec as P

F32 = jnp.float32
BF16 = jnp.bfloat16


def dot(a, b, ca, cb):
    return lax.dot_general(a, b, (((ca,), (cb,)), ((), ())), preferred_element_type=F32)


def xor_pairs(count, bits):
    return [(i, i ^ bits) for i in range(count)]


def with_partner(count, apart, value):
    branches = [
        functools.partial(lax.ppermute, axis_name="expert", perm=xor_pairs(count, bits))
        for bits in range(1, count)
    ]
    return lax.switch(apart - 1, branches, value)


def ring_gather(value, count):
    ring = [(i, (i + 2) % count) for i in range(count)]
    blocks = []
    for step in range(count // 2):
        if step > 0:
            value = lax.ppermute(value, "expert", ring)
        blocks += [value, lax.ppermute(value, "expert", xor_pairs(count, 1))]
    return jnp.concatenate(blocks, axis=0)


def ring_scatter(partial, count):
    rows = partial.shape[0] // count
    ring = [(i, (i + 2) % count) for i in range(count)]
    steps = count // 2
    twins = []
    for step in range(steps):
        at = ((step + 1) % steps * 2 + 1) * rows
        twins.append(lax.ppermute(partial[at : at + rows], "expert", xor_pairs(count, 1)))
    total = None
    for step in range(steps):
        at = (step + 1) % steps * 2 * rows
        own = partial[at : at + rows].astype(F32) + twins[step].astype(F32)
        if step > 0:
            own = own + lax.ppermute(total, "expert", ring).astype(F32)
        total = own.astype(BF16)
    return total


def after(value, *others):
    return lax.optimization_barrier((value, *others))[0]


def tile_of(extent, most):
    return max(t for t in range(128, most + 1, 128) if extent % t == 0)


def slot_matmul(slot, left, right, slots):
    rows, width = left.shape
    neurons = right.shape[1]
    tile = tile_of(width, 256)

    def kernel(slot_ref, left_ref, right_ref, out_ref):
        out_ref[0] = dot(left_ref[...], right_ref[...], 0, 0).astype(BF16)

    return pl.pallas_call(
        kernel,
        out_shape=jax.ShapeDtypeStruct((slots, width, neurons), BF16),
        grid_spec=pltpu.PrefetchScalarGridSpec(
            num_scalar_prefetch=1,
            grid=(width // tile,),
            in_specs=[
                pl.BlockSpec((rows, tile), lambda i, s: (0, i)),
                pl.BlockSpec((rows, neurons), lambda i, s: (0, 0)),
            ],
            out_specs=pl.BlockSpec((1, tile, neurons), lambda i, s: (s[0], i, 0)),
        ),
        compiler_params=pltpu.CompilerParams(vmem_limit_bytes=32 << 20),
        cost_estimate=pl.CostEstimate(
            flops=2 * rows * width * neurons,
            bytes_accessed=2 * (rows * width + rows * neurons + width * neurons),
            transcendentals=0,
        ),
    )(slot.reshape(1), left, right)


def slot_place(slot, keep, first, second, into):
    half, width = first.shape
    tile = tile_of(width, 256)

    def kernel(slot_ref, keep_ref, first_ref, second_ref, into_ref, out_ref):
        whole = jnp.concatenate([first_ref[...], second_ref[...]], axis=0).astype(F32)
        whole = jnp.where(keep_ref[0] > 0, whole, 0.0)
        out_ref[0] = whole.T.astype(BF16)

    return pl.pallas_call(
        kernel,
        out_shape=jax.ShapeDtypeStruct(into.shape, BF16),
        grid_spec=pltpu.PrefetchScalarGridSpec(
            num_scalar_prefetch=2,
            grid=(width // tile,),
            in_specs=[
                pl.BlockSpec((half, tile), lambda i, s, k: (0, i)),
                pl.BlockSpec((half, tile), lambda i, s, k: (0, i)),
                pl.BlockSpec(memory_space=pl.ANY),
            ],
            out_specs=pl.BlockSpec((1, tile, 2 * half), lambda i, s, k: (s[0], i, 0)),
        ),
        input_output_aliases={4: 0},
        compiler_params=pltpu.CompilerParams(vmem_limit_bytes=32 << 20),
        cost_estimate=pl.CostEstimate(
            flops=0, bytes_accessed=8 * half * width, transcendentals=0
        ),
    )(slot.reshape(1), keep.reshape(1), first, second, into)


def activations(gate_sum, up_sum, back_sum):
    sigma = jax.nn.sigmoid(gate_sum)
    active = gate_sum * sigma
    slope = sigma * (1.0 + gate_sum * (1.0 - sigma))
    return (
        (active * up_sum).astype(BF16),
        (back_sum * up_sum * slope).astype(BF16),
        (back_sum * active).astype(BF16),
    )


def shards(
    tokens,
    cotangent,
    gate_weight,
    up_weight,
    down_weight,
    routing,
    route_weight,
    merge_source,
    merge_target,
    neuron_perm,
):
    devices_n = lax.axis_size("expert")
    hidden_n = lax.axis_size("hidden")
    me = lax.axis_index("expert")
    low_bit = lax.axis_index("hidden") % 2
    exp_local, width, neurons = gate_weight.shape
    experts = exp_local * devices_n
    tok_local, top_count = routing.shape
    tok_all = tok_local * devices_n
    depth = max(2, tok_local * top_count * 4 // (3 * experts))
    slots = devices_n * depth
    half = neurons // 2
    weights = (gate_weight, up_weight, down_weight)

    source_dev = merge_source // exp_local
    target_dev = merge_target // exp_local
    is_source = source_dev == me
    is_target = target_dev == me
    mine = is_source | is_target
    am_target = jnp.any(is_target)
    partner = jnp.sum(jnp.where(is_source, target_dev, 0) + jnp.where(is_target, source_dev, 0))
    source_e = jnp.sum(jnp.where(mine, merge_source, 0))
    target_e = jnp.sum(jnp.where(mine, merge_target, 0))
    merged_slot = jnp.where(am_target, target_e, source_e) % exp_local
    other_slot = exp_local - 1 - merged_slot
    other_e = me * exp_local + other_slot
    perm = jnp.sum(jnp.where(mine[:, None], neuron_perm, 0), axis=0)

    expert_ids = jnp.arange(experts, dtype=jnp.int32)
    route = jnp.sum(
        jnp.where(routing[:, :, None] == expert_ids, route_weight[:, :, None], 0.0), axis=1
    )
    high = lax.reduce_precision(route, 8, 7)
    middle = lax.reduce_precision(route - high, 8, 7)
    low = route - high - middle
    pieces = jnp.concatenate([high, middle, low], axis=1).astype(BF16)
    pad = -pieces.shape[1] % 128
    payload = jnp.concatenate([tokens, jnp.pad(pieces, ((0, 0), (0, pad)))], axis=1)
    gathered = ring_gather(payload, devices_n)
    inputs_c = ring_gather(cotangent, devices_n)

    order = jnp.where(am_target, jnp.arange(neurons, dtype=jnp.int32), perm)
    keep_order = jnp.where(am_target, order[:half], order[half:])
    send_order = jnp.where(am_target, order[half:], order[:half])
    columns = jnp.arange(neurons, dtype=jnp.int32)
    keep_hot = (keep_order[:, None] == columns[None, :]).astype(BF16)
    send_hot = (send_order[:, None] == columns[None, :]).astype(BF16)
    chosen = [lax.dynamic_index_in_dim(w, merged_slot, 0, keepdims=False) for w in weights]
    others = [lax.dynamic_index_in_dim(w, other_slot, 0, keepdims=False) for w in weights]
    sends = [dot(send_hot, w, 1, 1).astype(BF16) for w in chosen]
    keeps = [dot(keep_hot, w, 1, 1).astype(BF16) for w in chosen]

    inputs_x = gathered[:, :width]
    parts = gathered[:, width : width + 3 * experts].astype(F32)
    route_all = parts[:, :experts] + parts[:, experts : 2 * experts] + parts[:, 2 * experts :]
    merged_hit = (expert_ids == source_e) | (expert_ids == target_e)
    merged_p = jnp.sum(jnp.where(merged_hit, route_all, 0.0), axis=1)
    other_p = jnp.sum(jnp.where(expert_ids == other_e, route_all, 0.0), axis=1)
    merged_dy = (merged_p[:, None] * inputs_c.astype(F32)).astype(BF16)

    named = (other_p > 0.0).reshape(devices_n, tok_local)
    upper = jnp.arange(tok_local)[:, None] <= jnp.arange(tok_local)[None, :]
    rank = dot(named.astype(BF16), upper.astype(BF16), 1, 0).astype(jnp.int32) - 1
    block = (jnp.arange(devices_n, dtype=jnp.int32) + (1 - low_bit) * (devices_n // 2)) % devices_n
    place = jnp.where(named, block[:, None] * depth + rank, -1).reshape(tok_all)
    slot_hot = jnp.arange(slots, dtype=jnp.int32)[:, None] == place[None, :]
    slot_p = jnp.sum(jnp.where(slot_hot, other_p[None, :], 0.0), axis=1)
    slot_hot = slot_hot.astype(BF16)
    other_x = dot(slot_hot, inputs_x, 1, 0).astype(BF16)
    other_dy = (dot(slot_hot, inputs_c, 1, 0) * slot_p[:, None]).astype(BF16)

    def core_sum(send_part, keep_part):
        if hidden_n == 1:
            return keep_part.astype(BF16)
        arrived = lax.ppermute(send_part.astype(BF16), "hidden", xor_pairs(hidden_n, 1))
        return (keep_part + arrived.astype(F32)).astype(BF16)

    def far_sum(part):
        total, bit = part.astype(F32), 2
        while bit < hidden_n:
            if bit > 2:
                part = total.astype(BF16)
            arrived = lax.ppermute(part, "hidden", xor_pairs(hidden_n, bit))
            total, bit = part.astype(F32) + arrived.astype(F32), bit * 2
        return total

    def swapped(value):
        return lax.ppermute(value, "hidden", xor_pairs(hidden_n, 1))

    slots_half = slots // 2
    quarter = half // 2
    apart = me ^ partner

    other_parts = [
        core_sum(dot(value[:slots_half], w, 1, 0), dot(value[slots_half:], w, 1, 0))
        for value, w in zip((other_x, other_x, other_dy), others)
    ]
    other_sums = [far_sum(part) for part in other_parts]

    last = other_parts
    merged, merged_sums = [], []
    for value, send, keep in zip((inputs_x, inputs_x, merged_dy), sends, keeps):
        arrived = with_partner(devices_n, apart, after(send, *last))
        w = (0.5 * (keep.astype(F32) + arrived.astype(F32))).astype(BF16)
        merged.append(w)
        w_send = lax.dynamic_slice_in_dim(w, (1 - low_bit) * quarter, quarter, 0)
        w_keep = lax.dynamic_slice_in_dim(w, low_bit * quarter, quarter, 0)
        part = core_sum(dot(w_send, value, 1, 1), dot(w_keep, value, 1, 1))
        merged_sums.append(far_sum(part))
        last = [part]

    other_h, other_dg, other_du = [
        jnp.concatenate([swapped(a), a], axis=0) for a in activations(*other_sums)
    ]
    other_y = (dot(other_h, others[2], 1, 1) * slot_p[:, None]).astype(BF16)
    other_mixed = dot(slot_hot, other_y, 0, 0)
    other_grads = [
        slot_matmul(other_slot, value, a, exp_local)
        for value, a in ((other_x, other_dg), (other_x, other_du), (other_dy, other_h))
    ]

    def ordered(a):
        b = swapped(a)
        return jnp.concatenate(
            [jnp.where(low_bit == 0, a, b), jnp.where(low_bit == 0, b, a)], axis=0
        )

    gate_sum, up_sum, back_sum = merged_sums
    sigma = jax.nn.sigmoid(gate_sum)
    active = gate_sum * sigma
    inner = up_sum * sigma * (1.0 + gate_sum * (1.0 - sigma))
    merged_h = ordered((active * up_sum).astype(BF16))
    mixed = other_mixed + merged_p[:, None] * dot(merged_h, merged[2], 0, 0)
    mixed = mixed.astype(BF16)
    down_half = dot(merged_h, merged_dy, 1, 0).astype(BF16)
    far_down = with_partner(devices_n, apart, after(down_half, mixed))
    mixed = ring_scatter(mixed, devices_n)
    gate_half = dot(ordered((back_sum * inner).astype(BF16)), inputs_x, 1, 0).astype(BF16)
    up_half = dot(ordered((back_sum * active).astype(BF16)), inputs_x, 1, 0).astype(BF16)
    far_gate, far_up = with_partner(devices_n, apart, (gate_half, up_half))

    keep_flag = am_target.astype(jnp.int32)
    outs = [
        slot_place(
            merged_slot,
            keep_flag,
            own,
            far,
            into,
        )
        for into, own, far in zip(
            other_grads, (gate_half, up_half, down_half), (far_gate, far_up, far_down)
        )
    ]
    return (mixed, *outs)


def solution(mesh):
    placed = (
        P("expert", "hidden"),
        P("expert", "hidden"),
        P("expert", "hidden", None),
        P("expert", "hidden", None),
        P("expert", "hidden", None),
        P("expert", None),
        P("expert", None),
        P(),
        P(),
        P(),
    )
    return jax.shard_map(
        shards,
        mesh=mesh,
        in_specs=placed,
        out_specs=(
            P("expert", "hidden"),
            P("expert", "hidden", None),
            P("expert", "hidden", None),
            P("expert", "hidden", None),
        ),
        check_vma=False,
    )
```

```python
import functools

import jax
import jax.numpy as jnp
from jax import lax
from jax.experimental import pallas as pl
from jax.experimental.pallas import tpu as pltpu
from jax.sharding import PartitionSpec as P

F32 = jnp.float32
BF16 = jnp.bfloat16


def dot(a, b, ca, cb):
    return lax.dot_general(a, b, (((ca,), (cb,)), ((), ())), preferred_element_type=F32)


def xor_pairs(count, bits):
    return [(i, i ^ bits) for i in range(count)]


def with_partner(count, apart, values, far=None, parts=()):
    def run(bits, values, parts):
        there = [lax.ppermute(v, "expert", xor_pairs(count, bits)) for v in values]
        return there, [far(part) for part in parts]

    branches = [functools.partial(run, bits) for bits in range(1, count)]
    return lax.switch(apart - 1, branches, list(values), list(parts))


def after(value, *others):
    return lax.optimization_barrier((value, *others))[0]


def ring_gather(value, count, beside):
    ring = [(i, (i + 2) % count) for i in range(count)]
    blocks = []
    for step in range(count // 2):
        if step > 0:
            value = after(lax.ppermute(value, "expert", ring), *beside[step - 1 :: count // 2 - 1])
        blocks += [value, lax.ppermute(value, "expert", xor_pairs(count, 1))]
    return jnp.concatenate(blocks, axis=0)


def ring_scatter(partial, count, later):
    rows = partial.shape[0] // count
    ring = [(i, (i + 2) % count) for i in range(count)]
    steps = count // 2
    twins = []
    for step in range(steps):
        at = ((step + 1) % steps * 2 + 1) * rows
        twins.append(lax.ppermute(partial[at : at + rows], "expert", xor_pairs(count, 1)))
    total = None
    for step in range(steps):
        at = (step + 1) % steps * 2 * rows
        own = partial[at : at + rows].astype(F32) + twins[step].astype(F32)
        if step > 0:
            own = own + lax.ppermute(total, "expert", ring).astype(F32)
        total = own.astype(BF16) if step > 0 else after(own.astype(BF16), later)
    return total


def tile_of(extent, most):
    return max(t for t in range(128, most + 1, 128) if extent % t == 0)


def slot_matmul(slot, left, right, slots):
    rows, width = left.shape
    neurons = right.shape[1]
    tile = tile_of(width, 256)

    def kernel(slot_ref, left_ref, right_ref, out_ref):
        out_ref[0] = dot(left_ref[...], right_ref[...], 0, 0).astype(BF16)

    return pl.pallas_call(
        kernel,
        out_shape=jax.ShapeDtypeStruct((slots, width, neurons), BF16),
        grid_spec=pltpu.PrefetchScalarGridSpec(
            num_scalar_prefetch=1,
            grid=(width // tile,),
            in_specs=[
                pl.BlockSpec((rows, tile), lambda i, s: (0, i)),
                pl.BlockSpec((rows, neurons), lambda i, s: (0, 0)),
            ],
            out_specs=pl.BlockSpec((1, tile, neurons), lambda i, s: (s[0], i, 0)),
        ),
        compiler_params=pltpu.CompilerParams(vmem_limit_bytes=32 << 20),
        cost_estimate=pl.CostEstimate(
            flops=2 * rows * width * neurons,
            bytes_accessed=2 * (rows * width + rows * neurons + width * neurons),
            transcendentals=0,
        ),
    )(slot.reshape(1), left, right)


def slot_place(slot, keep, swap, first, second, into):
    half, width = first.shape
    quarter = half // 2
    tile = tile_of(width, 256)

    def kernel(slot_ref, keep_ref, swap_ref, first_ref, second_ref, into_ref, out_ref):
        swap = swap_ref[0] > 0
        parts = []
        for ref in (first_ref, second_ref):
            one, two = ref[:quarter].astype(F32), ref[quarter:].astype(F32)
            parts += [jnp.where(swap, two, one), jnp.where(swap, one, two)]
        whole = jnp.concatenate(parts, axis=0)
        whole = jnp.where(keep_ref[0] > 0, whole, 0.0)
        out_ref[0] = whole.T.astype(BF16)

    return pl.pallas_call(
        kernel,
        out_shape=jax.ShapeDtypeStruct(into.shape, BF16),
        grid_spec=pltpu.PrefetchScalarGridSpec(
            num_scalar_prefetch=3,
            grid=(width // tile,),
            in_specs=[
                pl.BlockSpec((half, tile), lambda i, s, k, w: (0, i)),
                pl.BlockSpec((half, tile), lambda i, s, k, w: (0, i)),
                pl.BlockSpec(memory_space=pl.ANY),
            ],
            out_specs=pl.BlockSpec((1, tile, 2 * half), lambda i, s, k, w: (s[0], i, 0)),
        ),
        input_output_aliases={5: 0},
        compiler_params=pltpu.CompilerParams(vmem_limit_bytes=32 << 20),
        cost_estimate=pl.CostEstimate(
            flops=0, bytes_accessed=8 * half * width, transcendentals=0
        ),
    )(slot.reshape(1), keep.reshape(1), swap.reshape(1), first, second, into)


def activations(gate_sum, up_sum, back_sum):
    sigma = jax.nn.sigmoid(gate_sum)
    active = gate_sum * sigma
    slope = sigma * (1.0 + gate_sum * (1.0 - sigma))
    return (
        (active * up_sum).astype(BF16),
        (back_sum * up_sum * slope).astype(BF16),
        (back_sum * active).astype(BF16),
    )


def shards(
    tokens,
    cotangent,
    gate_weight,
    up_weight,
    down_weight,
    routing,
    route_weight,
    merge_source,
    merge_target,
    neuron_perm,
):
    devices_n = lax.axis_size("expert")
    hidden_n = lax.axis_size("hidden")
    me = lax.axis_index("expert")
    low_bit = lax.axis_index("hidden") % 2
    exp_local, width, neurons = gate_weight.shape
    experts = exp_local * devices_n
    tok_local, top_count = routing.shape
    tok_all = tok_local * devices_n
    depth = max(2, tok_local * top_count * 4 // (3 * experts))
    slots = devices_n * depth
    half = neurons // 2
    weights = (gate_weight, up_weight, down_weight)

    source_dev = merge_source // exp_local
    target_dev = merge_target // exp_local
    is_source = source_dev == me
    is_target = target_dev == me
    mine = is_source | is_target
    am_target = jnp.any(is_target)
    partner = jnp.sum(jnp.where(is_source, target_dev, 0) + jnp.where(is_target, source_dev, 0))
    source_e = jnp.sum(jnp.where(mine, merge_source, 0))
    target_e = jnp.sum(jnp.where(mine, merge_target, 0))
    merged_slot = jnp.where(am_target, target_e, source_e) % exp_local
    other_slot = exp_local - 1 - merged_slot
    other_e = me * exp_local + other_slot
    perm = jnp.sum(jnp.where(mine[:, None], neuron_perm, 0), axis=0)

    expert_ids = jnp.arange(experts, dtype=jnp.int32)
    route = jnp.sum(
        jnp.where(routing[:, :, None] == expert_ids, route_weight[:, :, None], 0.0), axis=1
    )
    high = lax.reduce_precision(route, 8, 7)
    middle = lax.reduce_precision(route - high, 8, 7)
    low = route - high - middle
    pieces = jnp.concatenate([high, middle, low], axis=1).astype(BF16)
    pad = -pieces.shape[1] % 128
    order = jnp.where(am_target, jnp.arange(neurons, dtype=jnp.int32), perm)
    order = order.reshape(2, 2, half // 2)
    order = jnp.where(low_bit == 0, order, order[:, ::-1]).reshape(2, half)
    keep_order = jnp.where(am_target, order[0], order[1])
    send_order = jnp.where(am_target, order[1], order[0])
    columns = jnp.arange(neurons, dtype=jnp.int32)
    keep_hot = (keep_order[:, None] == columns[None, :]).astype(BF16)
    send_hot = (send_order[:, None] == columns[None, :]).astype(BF16)
    chosen = [lax.dynamic_index_in_dim(w, merged_slot, 0, keepdims=False) for w in weights]
    others = [lax.dynamic_index_in_dim(w, other_slot, 0, keepdims=False) for w in weights]
    sends = [dot(send_hot, w, 1, 1).astype(BF16) for w in chosen]
    keeps = [dot(keep_hot, w, 1, 1).astype(BF16) for w in chosen]

    payload = jnp.concatenate([tokens, cotangent, jnp.pad(pieces, ((0, 0), (0, pad)))], axis=1)
    gathered = ring_gather(payload, devices_n, sends + keeps)
    inputs_x = gathered[:, :width]
    inputs_c = gathered[:, width : 2 * width]
    parts = gathered[:, 2 * width : 2 * width + 3 * experts].astype(F32)
    route_all = parts[:, :experts] + parts[:, experts : 2 * experts] + parts[:, 2 * experts :]
    merged_hit = (expert_ids == source_e) | (expert_ids == target_e)
    merged_p = jnp.sum(jnp.where(merged_hit, route_all, 0.0), axis=1)
    other_p = jnp.sum(jnp.where(expert_ids == other_e, route_all, 0.0), axis=1)
    merged_dy = (merged_p[:, None] * inputs_c.astype(F32)).astype(BF16)

    named = (other_p > 0.0).reshape(devices_n, tok_local)
    upper = jnp.arange(tok_local)[:, None] <= jnp.arange(tok_local)[None, :]
    rank = dot(named.astype(BF16), upper.astype(BF16), 1, 0).astype(jnp.int32) - 1
    block = (jnp.arange(devices_n, dtype=jnp.int32) + (1 - low_bit) * (devices_n // 2)) % devices_n
    place = jnp.where(named, block[:, None] * depth + rank, -1).reshape(tok_all)
    slot_hot = jnp.arange(slots, dtype=jnp.int32)[:, None] == place[None, :]
    slot_p = jnp.sum(jnp.where(slot_hot, other_p[None, :], 0.0), axis=1)
    slot_hot = slot_hot.astype(BF16)
    other_x = dot(slot_hot, inputs_x, 1, 0).astype(BF16)
    other_dy = (dot(slot_hot, inputs_c, 1, 0) * slot_p[:, None]).astype(BF16)

    def core_sum(send_part, keep_part):
        if hidden_n == 1:
            return keep_part.astype(BF16)
        arrived = lax.ppermute(send_part.astype(BF16), "hidden", xor_pairs(hidden_n, 1))
        return (keep_part + arrived.astype(F32)).astype(BF16)

    last_bit = 2
    while last_bit * 2 < hidden_n:
        last_bit *= 2

    def near_sum(part):
        bit = 2
        while bit < last_bit:
            arrived = lax.ppermute(part, "hidden", xor_pairs(hidden_n, bit))
            part, bit = (part.astype(F32) + arrived.astype(F32)).astype(BF16), bit * 2
        return part

    def far(part):
        if last_bit < hidden_n:
            return lax.ppermute(part, "hidden", xor_pairs(hidden_n, last_bit))
        return jnp.zeros_like(part)

    def added(one, two):
        return one.astype(F32) + two.astype(F32)

    def swapped(value):
        return lax.ppermute(value, "hidden", xor_pairs(hidden_n, 1))

    slots_half = slots // 2
    quarter = half // 2
    apart = me ^ partner

    other_parts = [
        near_sum(core_sum(dot(value[:slots_half], w, 1, 0), dot(value[slots_half:], w, 1, 0)))
        for value, w in zip((other_x, other_x, other_dy), others)
    ]

    arrived, other_far = with_partner(devices_n, apart, sends, far, other_parts)
    merged = [
        (0.5 * (k.astype(F32) + a.astype(F32))).astype(BF16) for k, a in zip(keeps, arrived)
    ]
    w_down = merged[2]
    merged_sums = []
    for value, w in zip((inputs_x, inputs_x, merged_dy), merged):
        part = near_sum(core_sum(dot(w[quarter:], value, 1, 1), dot(w[:quarter], value, 1, 1)))
        merged_sums.append((part, far(part)))

    other_h, other_dg, other_du = [
        jnp.concatenate([swapped(a), a], axis=0)
        for a in activations(*map(added, other_parts, other_far))
    ]
    other_y = (dot(other_h, others[2], 1, 1) * slot_p[:, None]).astype(BF16)
    other_mixed = dot(slot_hot, other_y, 0, 0)
    other_grads = [
        slot_matmul(other_slot, value, a, exp_local)
        for value, a in ((other_x, other_dg), (other_x, other_du), (other_dy, other_h))
    ]

    def joined(a):
        a = a.astype(BF16)
        return jnp.concatenate([a, swapped(a)], axis=0)

    gate_sum, up_sum = added(*merged_sums[0]), added(*merged_sums[1])
    sigma = jax.nn.sigmoid(gate_sum)
    active = gate_sum * sigma
    inner = up_sum * sigma * (1.0 + gate_sum * (1.0 - sigma))
    merged_h = joined(active * up_sum)
    mixed = (other_mixed + merged_p[:, None] * dot(merged_h, w_down, 0, 0)).astype(BF16)
    down_half = dot(merged_h, merged_dy, 1, 0).astype(BF16)
    (far_down,), _ = with_partner(devices_n, apart, [after(down_half, mixed)])
    mixed = ring_scatter(mixed, devices_n, far_down)
    back_sum = added(after(merged_sums[2][0], down_half), merged_sums[2][1])
    gate_half = dot(joined(back_sum * inner), inputs_x, 1, 0).astype(BF16)
    up_half = dot(joined(back_sum * active), inputs_x, 1, 0).astype(BF16)
    (far_gate, far_up), _ = with_partner(devices_n, apart, [gate_half, up_half])

    keep_flag = am_target.astype(jnp.int32)
    outs = [
        slot_place(
            merged_slot,
            keep_flag,
            low_bit,
            own,
            far,
            into,
        )
        for into, own, far in zip(
            other_grads, (gate_half, up_half, down_half), (far_gate, far_up, far_down)
        )
    ]
    return (mixed, *outs)


def solution(mesh):
    placed = (
        P("expert", "hidden"),
        P("expert", "hidden"),
        P("expert", "hidden", None),
        P("expert", "hidden", None),
        P("expert", "hidden", None),
        P("expert", None),
        P("expert", None),
        P(),
        P(),
        P(),
    )
    return jax.shard_map(
        shards,
        mesh=mesh,
        in_specs=placed,
        out_specs=(
            P("expert", "hidden"),
            P("expert", "hidden", None),
            P("expert", "hidden", None),
            P("expert", "hidden", None),
        ),
        check_vma=False,
    )
```

```python
import functools

import jax
import jax.numpy as jnp
from jax import lax
from jax.experimental import pallas as pl
from jax.experimental.pallas import tpu as pltpu
from jax.sharding import PartitionSpec as P

F32 = jnp.float32
BF16 = jnp.bfloat16


def dot(a, b, ca, cb):
    return lax.dot_general(a, b, (((ca,), (cb,)), ((), ())), preferred_element_type=F32)


def xor_pairs(count, bits):
    return [(i, i ^ bits) for i in range(count)]


def with_partner(count, apart, values, use, *others):
    def run(bits, values, *others):
        return use([lax.ppermute(v, "expert", xor_pairs(count, bits)) for v in values], *others)

    branches = [functools.partial(run, bits) for bits in range(1, count)]
    return lax.switch(apart - 1, branches, list(values), *others)


def after(value, *others):
    return lax.optimization_barrier((value, *others))[0]


def ring_gather(value, count):
    ring = [(i, (i + 2) % count) for i in range(count)]
    blocks = []
    for step in range(count // 2):
        if step > 0:
            value = lax.ppermute(value, "expert", ring)
        blocks += [value, lax.ppermute(value, "expert", xor_pairs(count, 1))]
    return jnp.concatenate(blocks, axis=0), blocks[2::2]


def ring_scatter(partial, count):
    rows = partial.shape[0] // count
    ring = [(i, (i + 2) % count) for i in range(count)]
    steps = count // 2
    twins = []
    for step in range(steps):
        at = ((step + 1) % steps * 2 + 1) * rows
        twins.append(lax.ppermute(partial[at : at + rows], "expert", xor_pairs(count, 1)))
    total = None
    for step in range(steps):
        at = (step + 1) % steps * 2 * rows
        own = partial[at : at + rows].astype(F32) + twins[step].astype(F32)
        if step > 0:
            own = own + lax.ppermute(total, "expert", ring).astype(F32)
        total = own.astype(BF16)
    return total


def tile_of(extent, most):
    return max(t for t in range(128, most + 1, 128) if extent % t == 0)


def slot_matmul(slot, left, right, slots):
    rows, width = left.shape
    neurons = right.shape[1]
    tile = tile_of(width, 256)

    def kernel(slot_ref, left_ref, right_ref, out_ref, done_ref):
        out_ref[0] = dot(left_ref[...], right_ref[...], 0, 0).astype(BF16)
        done_ref[...] = jnp.zeros_like(done_ref)

    return pl.pallas_call(
        kernel,
        out_shape=[
            jax.ShapeDtypeStruct((slots, width, neurons), BF16),
            jax.ShapeDtypeStruct((8, 128), F32),
        ],
        grid_spec=pltpu.PrefetchScalarGridSpec(
            num_scalar_prefetch=1,
            grid=(width // tile,),
            in_specs=[
                pl.BlockSpec((rows, tile), lambda i, s: (0, i)),
                pl.BlockSpec((rows, neurons), lambda i, s: (0, 0)),
            ],
            out_specs=[
                pl.BlockSpec((1, tile, neurons), lambda i, s: (s[0], i, 0)),
                pl.BlockSpec((8, 128), lambda i, s: (0, 0)),
            ],
        ),
        compiler_params=pltpu.CompilerParams(vmem_limit_bytes=32 << 20),
        cost_estimate=pl.CostEstimate(
            flops=2 * rows * width * neurons,
            bytes_accessed=2 * (rows * width + rows * neurons + width * neurons),
            transcendentals=0,
        ),
    )(slot.reshape(1), left, right)


def slot_place(slot, keep, swap, first, second, into):
    half, width = first.shape
    quarter = half // 2
    tile = tile_of(width, 256)

    def kernel(slot_ref, keep_ref, swap_ref, first_ref, second_ref, into_ref, out_ref):
        swap = swap_ref[0] > 0
        parts = []
        for ref in (first_ref, second_ref):
            one, two = ref[:quarter], ref[quarter:]
            parts += [jnp.where(swap, two, one), jnp.where(swap, one, two)]
        whole = jnp.concatenate(parts, axis=0)
        whole = jnp.where(keep_ref[0] > 0, whole, jnp.zeros((), BF16))
        out_ref[0] = whole.T

    return pl.pallas_call(
        kernel,
        out_shape=jax.ShapeDtypeStruct(into.shape, BF16),
        grid_spec=pltpu.PrefetchScalarGridSpec(
            num_scalar_prefetch=3,
            grid=(width // tile,),
            in_specs=[
                pl.BlockSpec((half, tile), lambda i, s, k, w: (0, i)),
                pl.BlockSpec((half, tile), lambda i, s, k, w: (0, i)),
                pl.BlockSpec(memory_space=pl.ANY),
            ],
            out_specs=pl.BlockSpec((1, tile, 2 * half), lambda i, s, k, w: (s[0], i, 0)),
        ),
        input_output_aliases={5: 0},
        compiler_params=pltpu.CompilerParams(vmem_limit_bytes=32 << 20),
        cost_estimate=pl.CostEstimate(
            flops=0, bytes_accessed=8 * half * width, transcendentals=0
        ),
    )(slot.reshape(1), keep.reshape(1), swap.reshape(1), first, second, into)


def hidden_units(gate_sum, up_sum):
    return (gate_sum * jax.nn.sigmoid(gate_sum) * up_sum,)


def hidden_gradients(gate_sum, up_sum, back_sum):
    sigma = jax.nn.sigmoid(gate_sum)
    slope = sigma * (1.0 + gate_sum * (1.0 - sigma))
    return back_sum * up_sum * slope, back_sum * (gate_sum * sigma)


def units_and_gradients(*sums):
    return *hidden_units(*sums[:2]), *hidden_gradients(*sums)


def elementwise(function, count, pairs, before=()):
    rows, cols = pairs[0][0].shape
    tile = max(t for t in range(16, 193, 16) if rows % t == 0)
    values = [value for pair in pairs for value in pair]

    def kernel(*refs):
        outs = refs[len(values) + len(before) :]

        def strip(i, carry):
            at = pl.ds(pl.multiple_of(i * 16, 16), 16)
            sums = [
                refs[2 * j][at, :].astype(F32) + refs[2 * j + 1][at, :].astype(F32)
                for j in range(len(pairs))
            ]
            for ref, result in zip(outs, function(*sums)):
                ref[at, :] = result.astype(BF16)
            return carry

        lax.fori_loop(0, tile // 16, strip, 0)

    spec = pl.BlockSpec((tile, cols), lambda i: (i, 0))
    return pl.pallas_call(
        kernel,
        out_shape=[jax.ShapeDtypeStruct((rows, cols), BF16)] * count,
        grid=(rows // tile,),
        in_specs=[spec] * len(values) + [pl.BlockSpec(memory_space=pl.ANY)] * len(before),
        out_specs=[spec] * count,
        compiler_params=pltpu.CompilerParams(vmem_limit_bytes=32 << 20),
        cost_estimate=pl.CostEstimate(
            flops=20 * rows * cols,
            bytes_accessed=2 * rows * cols * (len(values) + count),
            transcendentals=rows * cols,
        ),
    )(*values, *before)


def shards(
    tokens,
    cotangent,
    gate_weight,
    up_weight,
    down_weight,
    routing,
    route_weight,
    merge_source,
    merge_target,
    neuron_perm,
):
    devices_n = lax.axis_size("expert")
    hidden_n = lax.axis_size("hidden")
    me = lax.axis_index("expert")
    low_bit = lax.axis_index("hidden") % 2
    exp_local, width, neurons = gate_weight.shape
    experts = exp_local * devices_n
    tok_local, top_count = routing.shape
    tok_all = tok_local * devices_n
    depth = max(2, tok_local * top_count * 4 // (3 * experts))
    slots = devices_n * depth
    half = neurons // 2
    weights = (gate_weight, up_weight, down_weight)

    source_dev = merge_source // exp_local
    target_dev = merge_target // exp_local
    is_source = source_dev == me
    is_target = target_dev == me
    mine = is_source | is_target
    am_target = jnp.any(is_target)
    partner = jnp.sum(jnp.where(is_source, target_dev, 0) + jnp.where(is_target, source_dev, 0))
    source_e = jnp.sum(jnp.where(mine, merge_source, 0))
    target_e = jnp.sum(jnp.where(mine, merge_target, 0))
    merged_slot = jnp.where(am_target, target_e, source_e) % exp_local
    other_slot = exp_local - 1 - merged_slot
    other_e = me * exp_local + other_slot
    perm = jnp.sum(jnp.where(mine[:, None], neuron_perm, 0), axis=0)

    expert_ids = jnp.arange(experts, dtype=jnp.int32)
    route = jnp.sum(
        jnp.where(routing[:, :, None] == expert_ids, route_weight[:, :, None], 0.0), axis=1
    )
    high = lax.reduce_precision(route, 8, 7)
    middle = lax.reduce_precision(route - high, 8, 7)
    low = route - high - middle
    pieces = jnp.concatenate([high, middle, low], axis=1).astype(BF16)
    pad = -pieces.shape[1] % 128
    payload = jnp.concatenate([tokens, cotangent, jnp.pad(pieces, ((0, 0), (0, pad)))], axis=1)
    gathered, hops = ring_gather(payload, devices_n)

    order = jnp.where(am_target, jnp.arange(neurons, dtype=jnp.int32), perm)
    order = order.reshape(2, 2, half // 2)
    order = jnp.where(low_bit == 0, order, order[:, ::-1]).reshape(2, half)
    keep_order = jnp.where(am_target, order[0], order[1])
    send_order = jnp.where(am_target, order[1], order[0])
    columns = jnp.arange(neurons, dtype=jnp.int32)
    send_order = after(send_order, *hops[:1])
    keep_order = after(keep_order, *hops[1:2])
    keep_hot = (keep_order[:, None] == columns[None, :]).astype(BF16)
    send_hot = (send_order[:, None] == columns[None, :]).astype(BF16)
    chosen = [lax.dynamic_index_in_dim(w, merged_slot, 0, keepdims=False) for w in weights]
    others = [lax.dynamic_index_in_dim(w, other_slot, 0, keepdims=False) for w in weights]
    sends = [dot(send_hot, w, 1, 1).astype(BF16) for w in chosen]
    keeps = [dot(keep_hot, w, 1, 1).astype(BF16) for w in chosen]

    inputs_x = gathered[:, :width]
    inputs_c = gathered[:, width : 2 * width]
    parts = gathered[:, 2 * width : 2 * width + 3 * experts].astype(F32)
    route_all = parts[:, :experts] + parts[:, experts : 2 * experts] + parts[:, 2 * experts :]
    merged_hit = (expert_ids == source_e) | (expert_ids == target_e)
    merged_p = jnp.sum(jnp.where(merged_hit, route_all, 0.0), axis=1)
    other_p = jnp.sum(jnp.where(expert_ids == other_e, route_all, 0.0), axis=1)
    merged_dy = (merged_p[:, None] * inputs_c.astype(F32)).astype(BF16)

    named = (other_p > 0.0).reshape(devices_n, tok_local)
    upper = jnp.arange(tok_local)[:, None] <= jnp.arange(tok_local)[None, :]
    rank = dot(named.astype(BF16), upper.astype(BF16), 1, 0).astype(jnp.int32) - 1
    block = (jnp.arange(devices_n, dtype=jnp.int32) + (1 - low_bit) * (devices_n // 2)) % devices_n
    place = jnp.where(named, block[:, None] * depth + rank, -1).reshape(tok_all)
    slot_hot = jnp.arange(slots, dtype=jnp.int32)[:, None] == place[None, :]
    slot_p = jnp.sum(jnp.where(slot_hot, other_p[None, :], 0.0), axis=1)
    slot_hot = slot_hot.astype(BF16)
    other_x = dot(slot_hot, inputs_x, 1, 0).astype(BF16)
    other_dy = (dot(slot_hot, inputs_c, 1, 0) * slot_p[:, None]).astype(BF16)

    def core_sum(send_part, keep_part):
        if hidden_n == 1:
            return keep_part.astype(BF16)
        arrived = lax.ppermute(send_part.astype(BF16), "hidden", xor_pairs(hidden_n, 1))
        return (keep_part + arrived.astype(F32)).astype(BF16)

    last_bit = 2
    while last_bit * 2 < hidden_n:
        last_bit *= 2

    def near_sum(part):
        bit = 2
        while bit < last_bit:
            arrived = lax.ppermute(part, "hidden", xor_pairs(hidden_n, bit))
            part, bit = (part.astype(F32) + arrived.astype(F32)).astype(BF16), bit * 2
        return part

    def far(part):
        if last_bit < hidden_n:
            return lax.ppermute(part, "hidden", xor_pairs(hidden_n, last_bit))
        return jnp.zeros_like(part)

    def swapped(value):
        return lax.ppermute(value, "hidden", xor_pairs(hidden_n, 1))

    slots_half = slots // 2
    quarter = half // 2

    other_parts = [
        near_sum(core_sum(dot(value[:slots_half], w, 1, 0), dot(value[slots_half:], w, 1, 0)))
        for value, w in zip((other_x, other_x, other_dy), others)
    ]

    def blend(arrived, keeps, parts):
        crossed = [far(part) for part in parts]
        merged = [
            (0.5 * (k.astype(F32) + a.astype(F32))).astype(BF16) for k, a in zip(keeps, arrived)
        ]
        return merged, crossed

    merged, other_far = with_partner(devices_n, me ^ partner, sends, blend, keeps, other_parts)
    w_down = merged[2]
    merged_sums = []
    for value, w in zip((inputs_x, inputs_x, merged_dy), merged):
        part = near_sum(core_sum(dot(w[quarter:], value, 1, 1), dot(w[:quarter], value, 1, 1)))
        merged_sums.append((part, far(part)))

    other_h, other_dg, other_du = [
        jnp.concatenate([swapped(a), a], axis=0)
        for a in elementwise(units_and_gradients, 3, list(zip(other_parts, other_far)))
    ]
    other_y = (dot(other_h, others[2], 1, 1) * slot_p[:, None]).astype(BF16)
    other_mixed = dot(slot_hot, other_y, 0, 0)
    other_grads, other_done = zip(*[
        slot_matmul(other_slot, value, a, exp_local)
        for value, a in ((other_x, other_dg), (other_x, other_du), (other_dy, other_h))
    ])

    def joined(a):
        return jnp.concatenate([a, swapped(a)], axis=0)

    (merged_h,) = elementwise(
        hidden_units, 1, merged_sums[:2], before=(other_mixed, merged_sums[2][0], *other_done)
    )
    merged_h = joined(merged_h)
    mixed = (other_mixed + merged_p[:, None] * dot(merged_h, w_down, 0, 0)).astype(BF16)
    down_half = dot(merged_h, merged_dy, 1, 0).astype(BF16)
    mixed = ring_scatter(mixed, devices_n)
    merged_dg, merged_du = elementwise(hidden_gradients, 2, merged_sums)
    gate_half = dot(joined(merged_dg), inputs_x, 1, 0).astype(BF16)
    up_half = dot(joined(merged_du), inputs_x, 1, 0).astype(BF16)
    far_gate, far_up, far_down = with_partner(
        devices_n, me ^ partner, [gate_half, up_half, down_half], list
    )

    keep_flag = am_target.astype(jnp.int32)
    outs = [
        slot_place(
            merged_slot,
            keep_flag,
            low_bit,
            own,
            far,
            into,
        )
        for into, own, far in zip(
            other_grads, (gate_half, up_half, down_half), (far_gate, far_up, far_down)
        )
    ]
    return (mixed, *outs)


def solution(mesh):
    placed = (
        P("expert", "hidden"),
        P("expert", "hidden"),
        P("expert", "hidden", None),
        P("expert", "hidden", None),
        P("expert", "hidden", None),
        P("expert", None),
        P("expert", None),
        P(),
        P(),
        P(),
    )
    return jax.shard_map(
        shards,
        mesh=mesh,
        in_specs=placed,
        out_specs=(
            P("expert", "hidden"),
            P("expert", "hidden", None),
            P("expert", "hidden", None),
            P("expert", "hidden", None),
        ),
        check_vma=False,
    )
```

```python
import functools

import jax
import jax.numpy as jnp
from jax import lax
from jax.experimental import pallas as pl
from jax.experimental.pallas import tpu as pltpu
from jax.sharding import PartitionSpec as P

F32 = jnp.float32
BF16 = jnp.bfloat16


def dot(a, b, ca, cb):
    return lax.dot_general(a, b, (((ca,), (cb,)), ((), ())), preferred_element_type=F32)


def xor_pairs(count, bits):
    return [(i, i ^ bits) for i in range(count)]


def with_partner(count, apart, values, use, *others):
    def run(bits, values, *others):
        return use([lax.ppermute(v, "expert", xor_pairs(count, bits)) for v in values], *others)

    branches = [functools.partial(run, bits) for bits in range(1, count)]
    return lax.switch(apart - 1, branches, list(values), *others)


def never(value):
    return (value[0, 0] > 1e30).astype(jnp.int32)


def ring_gather(value, count):
    ring = [(i, (i + 2) % count) for i in range(count)]
    blocks = []
    for step in range(count // 2):
        if step > 0:
            value = lax.ppermute(value, "expert", ring)
        blocks += [value, lax.ppermute(value, "expert", xor_pairs(count, 1))]
    return jnp.concatenate(blocks, axis=0), blocks[2::2] or blocks[:1]


def ring_scatter(partial, count, later):
    rows = partial.shape[0] // count
    ring = [(i, (i + 2) % count) for i in range(count)]
    steps = count // 2
    twins = []
    for step in range(steps):
        at = ((step + 1) % steps * 2 + 1) * rows
        twins.append(lax.ppermute(partial[at : at + rows], "expert", xor_pairs(count, 1)))
    total = None
    for step in range(steps):
        at = (step + 1) % steps * 2 * rows
        own = partial[at : at + rows].astype(F32) + twins[step].astype(F32)
        if step > 0:
            own = own + lax.ppermute(total, "expert", ring).astype(F32)
        if step == 1:
            own = own + never(later)
        total = own.astype(BF16)
    return total


def tile_of(extent, most):
    return max(t for t in range(128, most + 1, 128) if extent % t == 0)


def slot_matmul(slot, left, right, slots):
    rows, width = left.shape
    neurons = right.shape[1]
    tile = tile_of(width, 256)

    def kernel(slot_ref, left_ref, right_ref, out_ref, done_ref):
        out_ref[0] = dot(left_ref[...], right_ref[...], 0, 0).astype(BF16)
        done_ref[...] = jnp.zeros_like(done_ref)

    return pl.pallas_call(
        kernel,
        out_shape=[
            jax.ShapeDtypeStruct((slots, width, neurons), BF16),
            jax.ShapeDtypeStruct((8, 128), F32),
        ],
        grid_spec=pltpu.PrefetchScalarGridSpec(
            num_scalar_prefetch=1,
            grid=(width // tile,),
            in_specs=[
                pl.BlockSpec((rows, tile), lambda i, s: (0, i)),
                pl.BlockSpec((rows, neurons), lambda i, s: (0, 0)),
            ],
            out_specs=[
                pl.BlockSpec((1, tile, neurons), lambda i, s: (s[0], i, 0)),
                pl.BlockSpec((8, 128), lambda i, s: (0, 0)),
            ],
        ),
        compiler_params=pltpu.CompilerParams(vmem_limit_bytes=32 << 20),
        cost_estimate=pl.CostEstimate(
            flops=2 * rows * width * neurons,
            bytes_accessed=2 * (rows * width + rows * neurons + width * neurons),
            transcendentals=0,
        ),
    )(slot.reshape(1), left, right)


def slot_place(slot, keep, swap, first, second, into):
    half, width = first.shape
    quarter = half // 2
    tile = tile_of(width, 256)

    def kernel(slot_ref, keep_ref, swap_ref, first_ref, second_ref, into_ref, out_ref):
        swap = swap_ref[0] > 0
        parts = []
        for ref in (first_ref, second_ref):
            one, two = ref[:quarter], ref[quarter:]
            parts += [jnp.where(swap, two, one), jnp.where(swap, one, two)]
        whole = jnp.concatenate(parts, axis=0)
        whole = jnp.where(keep_ref[0] > 0, whole, jnp.zeros((), BF16))
        out_ref[0] = whole.T

    return pl.pallas_call(
        kernel,
        out_shape=jax.ShapeDtypeStruct(into.shape, BF16),
        grid_spec=pltpu.PrefetchScalarGridSpec(
            num_scalar_prefetch=3,
            grid=(width // tile,),
            in_specs=[
                pl.BlockSpec((half, tile), lambda i, s, k, w: (0, i)),
                pl.BlockSpec((half, tile), lambda i, s, k, w: (0, i)),
                pl.BlockSpec(memory_space=pl.ANY),
            ],
            out_specs=pl.BlockSpec((1, tile, 2 * half), lambda i, s, k, w: (s[0], i, 0)),
        ),
        input_output_aliases={5: 0},
        compiler_params=pltpu.CompilerParams(vmem_limit_bytes=32 << 20),
        cost_estimate=pl.CostEstimate(
            flops=0, bytes_accessed=8 * half * width, transcendentals=0
        ),
    )(slot.reshape(1), keep.reshape(1), swap.reshape(1), first, second, into)


def mean(total):
    return (0.5 * total,)


def hidden_units(gate_sum, up_sum):
    return (gate_sum * jax.nn.sigmoid(gate_sum) * up_sum,)


def hidden_gradients(gate_sum, up_sum, back_sum):
    sigma = jax.nn.sigmoid(gate_sum)
    slope = sigma * (1.0 + gate_sum * (1.0 - sigma))
    return back_sum * up_sum * slope, back_sum * (gate_sum * sigma)


def units_and_gradients(*sums):
    return *hidden_units(*sums[:2]), *hidden_gradients(*sums)


def elementwise(function, count, pairs, before=()):
    rows, cols = pairs[0][0].shape
    tile = max(t for t in range(16, 193, 16) if rows % t == 0)
    values = [value for pair in pairs for value in pair]

    def kernel(*refs):
        outs = refs[len(values) + len(before) :]

        def strip(i, carry):
            at = pl.ds(pl.multiple_of(i * 16, 16), 16)
            sums = [
                refs[2 * j][at, :].astype(F32) + refs[2 * j + 1][at, :].astype(F32)
                for j in range(len(pairs))
            ]
            for ref, result in zip(outs, function(*sums)):
                ref[at, :] = result.astype(BF16)
            return carry

        lax.fori_loop(0, tile // 16, strip, 0)

    spec = pl.BlockSpec((tile, cols), lambda i: (i, 0))
    return pl.pallas_call(
        kernel,
        out_shape=[jax.ShapeDtypeStruct((rows, cols), BF16)] * count,
        grid=(rows // tile,),
        in_specs=[spec] * len(values) + [pl.BlockSpec(memory_space=pl.ANY)] * len(before),
        out_specs=[spec] * count,
        compiler_params=pltpu.CompilerParams(vmem_limit_bytes=32 << 20),
        cost_estimate=pl.CostEstimate(
            flops=20 * rows * cols,
            bytes_accessed=2 * rows * cols * (len(values) + count),
            transcendentals=rows * cols,
        ),
    )(*values, *before)


def shards(
    tokens,
    cotangent,
    gate_weight,
    up_weight,
    down_weight,
    routing,
    route_weight,
    merge_source,
    merge_target,
    neuron_perm,
):
    devices_n = lax.axis_size("expert")
    hidden_n = lax.axis_size("hidden")
    me = lax.axis_index("expert")
    low_bit = lax.axis_index("hidden") % 2
    exp_local, width, neurons = gate_weight.shape
    experts = exp_local * devices_n
    tok_local, top_count = routing.shape
    tok_all = tok_local * devices_n
    depth = max(2, tok_local * top_count * 4 // (3 * experts))
    slots = devices_n * depth
    half = neurons // 2
    weights = (gate_weight, up_weight, down_weight)

    expert_ids = jnp.arange(experts, dtype=jnp.int32)
    route = jnp.sum(
        jnp.where(routing[:, :, None] == expert_ids, route_weight[:, :, None], 0.0), axis=1
    )
    high = lax.reduce_precision(route, 8, 7)
    middle = lax.reduce_precision(route - high, 8, 7)
    low = route - high - middle
    pieces = jnp.concatenate([high, middle, low], axis=1).astype(BF16)
    pad = -pieces.shape[1] % 128
    payload = jnp.concatenate([tokens, cotangent, jnp.pad(pieces, ((0, 0), (0, pad)))], axis=1)
    gathered, hops = ring_gather(payload, devices_n)

    merge_source = merge_source + never(hops[0])
    source_dev = merge_source // exp_local
    target_dev = merge_target // exp_local
    is_source = source_dev == me
    is_target = target_dev == me
    mine = is_source | is_target
    am_target = jnp.any(is_target)
    partner = jnp.sum(jnp.where(is_source, target_dev, 0) + jnp.where(is_target, source_dev, 0))
    source_e = jnp.sum(jnp.where(mine, merge_source, 0))
    target_e = jnp.sum(jnp.where(mine, merge_target, 0))
    merged_slot = jnp.where(am_target, target_e, source_e) % exp_local
    other_slot = exp_local - 1 - merged_slot
    other_e = me * exp_local + other_slot
    perm = jnp.sum(jnp.where(mine[:, None], neuron_perm, 0), axis=0)

    order = jnp.where(am_target, jnp.arange(neurons, dtype=jnp.int32), perm)
    order = order.reshape(2, 2, half // 2)
    order = jnp.where(low_bit == 0, order, order[:, ::-1]).reshape(2, half)
    keep_order = jnp.where(am_target, order[0], order[1])
    send_order = jnp.where(am_target, order[1], order[0])
    columns = jnp.arange(neurons, dtype=jnp.int32)
    keep_hot = (keep_order[:, None] == columns[None, :]).astype(BF16)
    send_hot = (send_order[:, None] == columns[None, :]).astype(BF16)
    chosen = [lax.dynamic_index_in_dim(w, merged_slot, 0, keepdims=False) for w in weights]
    others = [lax.dynamic_index_in_dim(w, other_slot, 0, keepdims=False) for w in weights]
    sends = [dot(send_hot, w, 1, 1).astype(BF16) for w in chosen]
    keeps = [dot(keep_hot, w, 1, 1).astype(BF16) for w in chosen]

    inputs_x = gathered[:, :width]
    inputs_c = gathered[:, width : 2 * width]
    parts = gathered[:, 2 * width : 2 * width + 3 * experts].astype(F32)
    route_all = parts[:, :experts] + parts[:, experts : 2 * experts] + parts[:, 2 * experts :]
    merged_hit = (expert_ids == source_e) | (expert_ids == target_e)
    merged_p = jnp.sum(jnp.where(merged_hit, route_all, 0.0), axis=1)
    other_p = jnp.sum(jnp.where(expert_ids == other_e, route_all, 0.0), axis=1)
    merged_dy = (merged_p[:, None] * inputs_c.astype(F32)).astype(BF16)

    named = (other_p > 0.0).reshape(devices_n, tok_local)
    upper = jnp.arange(tok_local)[:, None] <= jnp.arange(tok_local)[None, :]
    rank = dot(named.astype(BF16), upper.astype(BF16), 1, 0).astype(jnp.int32) - 1
    block = (jnp.arange(devices_n, dtype=jnp.int32) + (1 - low_bit) * (devices_n // 2)) % devices_n
    place = jnp.where(named, block[:, None] * depth + rank, -1).reshape(tok_all)
    slot_hot = jnp.arange(slots, dtype=jnp.int32)[:, None] == place[None, :]
    slot_p = jnp.sum(jnp.where(slot_hot, other_p[None, :], 0.0), axis=1)
    slot_hot = slot_hot.astype(BF16)
    other_x = dot(slot_hot, inputs_x, 1, 0).astype(BF16)
    other_dy = (dot(slot_hot, inputs_c, 1, 0) * slot_p[:, None]).astype(BF16)

    def core_sum(send_part, keep_part):
        if hidden_n == 1:
            return keep_part.astype(BF16)
        arrived = lax.ppermute(send_part.astype(BF16), "hidden", xor_pairs(hidden_n, 1))
        return (keep_part + arrived.astype(F32)).astype(BF16)

    last_bit = 2
    while last_bit * 2 < hidden_n:
        last_bit *= 2

    def near_sum(part):
        bit = 2
        while bit < last_bit:
            arrived = lax.ppermute(part, "hidden", xor_pairs(hidden_n, bit))
            part, bit = (part.astype(F32) + arrived.astype(F32)).astype(BF16), bit * 2
        return part

    def far(part):
        if last_bit < hidden_n:
            return lax.ppermute(part, "hidden", xor_pairs(hidden_n, last_bit))
        return jnp.zeros_like(part)

    def swapped(value):
        return lax.ppermute(value, "hidden", xor_pairs(hidden_n, 1))

    slots_half = slots // 2
    quarter = half // 2

    other_parts = [
        near_sum(core_sum(dot(value[:slots_half], w, 1, 0), dot(value[slots_half:], w, 1, 0)))
        for value, w in zip((other_x, other_x, other_dy), others)
    ]

    def blend(arrived, keeps, parts):
        crossed = [far(part) for part in parts]
        merged = [elementwise(mean, 1, [pair])[0] for pair in zip(keeps, arrived)]
        return merged, crossed

    merged, other_far = with_partner(devices_n, me ^ partner, sends, blend, keeps, other_parts)
    w_down = merged[2]
    merged_sums = []
    for value, w in zip((inputs_x, inputs_x, merged_dy), merged):
        part = near_sum(core_sum(dot(w[quarter:], value, 1, 1), dot(w[:quarter], value, 1, 1)))
        merged_sums.append((part, far(part)))

    other_h, other_dg, other_du = [
        jnp.concatenate([swapped(a), a], axis=0)
        for a in elementwise(units_and_gradients, 3, list(zip(other_parts, other_far)))
    ]
    other_y = (dot(other_h, others[2], 1, 1) * slot_p[:, None]).astype(BF16)
    other_mixed = dot(slot_hot, other_y, 0, 0)
    other_grads, other_done = zip(*[
        slot_matmul(other_slot, value, a, exp_local)
        for value, a in ((other_x, other_dg), (other_x, other_du), (other_dy, other_h))
    ])

    def joined(a):
        return jnp.concatenate([a, swapped(a)], axis=0)

    merged_h, merged_dg, merged_du = map(
        joined,
        elementwise(units_and_gradients, 3, merged_sums, before=(other_mixed, *other_done)),
    )
    mixed = (other_mixed + merged_p[:, None] * dot(merged_h, w_down, 0, 0)).astype(BF16)
    halves = [
        dot(a, value, 1, 0).astype(BF16)
        for a, value in ((merged_dg, inputs_x), (merged_du, inputs_x), (merged_h, merged_dy))
    ]
    far_halves = with_partner(devices_n, me ^ partner, halves, list)
    mixed = ring_scatter(mixed, devices_n, far_halves[0])

    keep_flag = am_target.astype(jnp.int32)
    outs = [
        slot_place(
            merged_slot,
            keep_flag,
            low_bit,
            own,
            far,
            into,
        )
        for into, own, far in zip(
            other_grads, halves, far_halves
        )
    ]
    return (mixed, *outs)


def solution(mesh):
    placed = (
        P("expert", "hidden"),
        P("expert", "hidden"),
        P("expert", "hidden", None),
        P("expert", "hidden", None),
        P("expert", "hidden", None),
        P("expert", None),
        P("expert", None),
        P(),
        P(),
        P(),
    )
    return jax.shard_map(
        shards,
        mesh=mesh,
        in_specs=placed,
        out_specs=(
            P("expert", "hidden"),
            P("expert", "hidden", None),
            P("expert", "hidden", None),
            P("expert", "hidden", None),
        ),
        check_vma=False,
    )
```

```python
import functools

import jax
import jax.numpy as jnp
from jax import lax
from jax.experimental import pallas as pl
from jax.experimental.pallas import tpu as pltpu
from jax.sharding import PartitionSpec as P

F32 = jnp.float32
BF16 = jnp.bfloat16


def dot(a, b, ca, cb):
    return lax.dot_general(a, b, (((ca,), (cb,)), ((), ())), preferred_element_type=F32)


def xor_pairs(count, bits):
    return [(i, i ^ bits) for i in range(count)]


def with_partner(count, apart, values, use, *others):
    def run(bits, values, *others):
        return use([lax.ppermute(v, "expert", xor_pairs(count, bits)) for v in values], *others)

    branches = [functools.partial(run, bits) for bits in range(1, count)]
    return lax.switch(apart - 1, branches, list(values), *others)


def ring_gather(value, count):
    ring = [(i, (i + 2) % count) for i in range(count)]
    blocks = []
    for step in range(count // 2):
        if step > 0:
            value = lax.ppermute(value, "expert", ring)
        blocks += [value, lax.ppermute(value, "expert", xor_pairs(count, 1))]
    return jnp.concatenate(blocks, axis=0)


def ring_scatter(partial, count):
    rows = partial.shape[0] // count
    ring = [(i, (i + 2) % count) for i in range(count)]
    steps = count // 2
    twins = []
    for step in range(steps):
        at = ((step + 1) % steps * 2 + 1) * rows
        twins.append(lax.ppermute(partial[at : at + rows], "expert", xor_pairs(count, 1)))
    totals = []
    for step in range(steps):
        at = (step + 1) % steps * 2 * rows
        own = partial[at : at + rows].astype(F32) + twins[step].astype(F32)
        if step > 0:
            own = own + lax.ppermute(totals[-1], "expert", ring).astype(F32)
        totals.append(own.astype(BF16))
    return totals[-1], totals


def tile_of(extent, most):
    return max(t for t in range(128, most + 1, 128) if extent % t == 0)


def slot_matmul(slot, left, right, slots):
    rows, width = left.shape
    neurons = right.shape[1]
    tile = tile_of(width, 256)

    def kernel(slot_ref, left_ref, right_ref, out_ref, done_ref):
        out_ref[0] = dot(left_ref[...], right_ref[...], 0, 0).astype(BF16)
        done_ref[...] = jnp.zeros_like(done_ref)

    return pl.pallas_call(
        kernel,
        out_shape=[
            jax.ShapeDtypeStruct((slots, width, neurons), BF16),
            jax.ShapeDtypeStruct((8, 128), F32),
        ],
        grid_spec=pltpu.PrefetchScalarGridSpec(
            num_scalar_prefetch=1,
            grid=(width // tile,),
            in_specs=[
                pl.BlockSpec((rows, tile), lambda i, s: (0, i)),
                pl.BlockSpec((rows, neurons), lambda i, s: (0, 0)),
            ],
            out_specs=[
                pl.BlockSpec((1, tile, neurons), lambda i, s: (s[0], i, 0)),
                pl.BlockSpec((8, 128), lambda i, s: (0, 0)),
            ],
        ),
        compiler_params=pltpu.CompilerParams(vmem_limit_bytes=32 << 20),
        cost_estimate=pl.CostEstimate(
            flops=2 * rows * width * neurons,
            bytes_accessed=2 * (rows * width + rows * neurons + width * neurons),
            transcendentals=0,
        ),
    )(slot.reshape(1), left, right)


def slot_place(slot, keep, swap, first, second, into):
    half, width = first.shape
    quarter = half // 2
    tile = tile_of(width, 256)

    def kernel(slot_ref, keep_ref, swap_ref, first_ref, second_ref, into_ref, out_ref):
        swap = swap_ref[0] > 0
        parts = []
        for ref in (first_ref, second_ref):
            one, two = ref[:quarter], ref[quarter:]
            parts += [jnp.where(swap, two, one), jnp.where(swap, one, two)]
        whole = jnp.concatenate(parts, axis=0)
        whole = jnp.where(keep_ref[0] > 0, whole, jnp.zeros((), BF16))
        out_ref[0] = whole.T

    return pl.pallas_call(
        kernel,
        out_shape=jax.ShapeDtypeStruct(into.shape, BF16),
        grid_spec=pltpu.PrefetchScalarGridSpec(
            num_scalar_prefetch=3,
            grid=(width // tile,),
            in_specs=[
                pl.BlockSpec((half, tile), lambda i, s, k, w: (0, i)),
                pl.BlockSpec((half, tile), lambda i, s, k, w: (0, i)),
                pl.BlockSpec(memory_space=pl.ANY),
            ],
            out_specs=pl.BlockSpec((1, tile, 2 * half), lambda i, s, k, w: (s[0], i, 0)),
        ),
        input_output_aliases={5: 0},
        compiler_params=pltpu.CompilerParams(vmem_limit_bytes=32 << 20),
        cost_estimate=pl.CostEstimate(
            flops=0, bytes_accessed=8 * half * width, transcendentals=0
        ),
    )(slot.reshape(1), keep.reshape(1), swap.reshape(1), first, second, into)


def mean(total):
    return (0.5 * total,)


def hidden_units(gate_sum, up_sum):
    return (gate_sum * jax.nn.sigmoid(gate_sum) * up_sum,)


def hidden_gradients(gate_sum, up_sum, back_sum):
    sigma = jax.nn.sigmoid(gate_sum)
    slope = sigma * (1.0 + gate_sum * (1.0 - sigma))
    return back_sum * up_sum * slope, back_sum * (gate_sum * sigma)


def units_and_gradients(*sums):
    return *hidden_units(*sums[:2]), *hidden_gradients(*sums)


def elementwise(function, count, pairs, before=()):
    rows, cols = pairs[0][0].shape
    tile = max(t for t in range(16, 193, 16) if rows % t == 0)
    values = [value for pair in pairs for value in pair]

    def kernel(*refs):
        outs = refs[len(values) + len(before) :]

        def strip(i, carry):
            at = pl.ds(pl.multiple_of(i * 16, 16), 16)
            sums = [
                refs[2 * j][at, :].astype(F32) + refs[2 * j + 1][at, :].astype(F32)
                for j in range(len(pairs))
            ]
            for ref, result in zip(outs, function(*sums)):
                ref[at, :] = result.astype(BF16)
            return carry

        lax.fori_loop(0, tile // 16, strip, 0)

    spec = pl.BlockSpec((tile, cols), lambda i: (i, 0))
    return pl.pallas_call(
        kernel,
        out_shape=[jax.ShapeDtypeStruct((rows, cols), BF16)] * count,
        grid=(rows // tile,),
        in_specs=[spec] * len(values) + [pl.BlockSpec(memory_space=pl.ANY)] * len(before),
        out_specs=[spec] * count,
        compiler_params=pltpu.CompilerParams(vmem_limit_bytes=32 << 20),
        cost_estimate=pl.CostEstimate(
            flops=20 * rows * cols,
            bytes_accessed=2 * rows * cols * (len(values) + count),
            transcendentals=rows * cols,
        ),
    )(*values, *before)


def shards(
    tokens,
    cotangent,
    gate_weight,
    up_weight,
    down_weight,
    routing,
    route_weight,
    merge_source,
    merge_target,
    neuron_perm,
):
    devices_n = lax.axis_size("expert")
    hidden_n = lax.axis_size("hidden")
    me = lax.axis_index("expert")
    low_bit = lax.axis_index("hidden") % 2
    exp_local, width, neurons = gate_weight.shape
    experts = exp_local * devices_n
    tok_local, top_count = routing.shape
    tok_all = tok_local * devices_n
    depth = max(2, tok_local * top_count * 4 // (3 * experts))
    slots = devices_n * depth
    half = neurons // 2
    weights = (gate_weight, up_weight, down_weight)

    expert_ids = jnp.arange(experts, dtype=jnp.int32)
    route = jnp.sum(
        jnp.where(routing[:, :, None] == expert_ids, route_weight[:, :, None], 0.0), axis=1
    )
    high = lax.reduce_precision(route, 8, 7)
    middle = lax.reduce_precision(route - high, 8, 7)
    low = route - high - middle
    pieces = jnp.concatenate([high, middle, low], axis=1).astype(BF16)
    pad = -pieces.shape[1] % 128
    payload = jnp.concatenate([tokens, cotangent, jnp.pad(pieces, ((0, 0), (0, pad)))], axis=1)
    gathered = ring_gather(payload, devices_n)

    source_dev = merge_source // exp_local
    target_dev = merge_target // exp_local
    is_source = source_dev == me
    is_target = target_dev == me
    mine = is_source | is_target
    am_target = jnp.any(is_target)
    partner = jnp.sum(jnp.where(is_source, target_dev, 0) + jnp.where(is_target, source_dev, 0))
    source_e = jnp.sum(jnp.where(mine, merge_source, 0))
    target_e = jnp.sum(jnp.where(mine, merge_target, 0))
    merged_slot = jnp.where(am_target, target_e, source_e) % exp_local
    other_slot = exp_local - 1 - merged_slot
    other_e = me * exp_local + other_slot
    perm = jnp.sum(jnp.where(mine[:, None], neuron_perm, 0), axis=0)

    order = jnp.where(am_target, jnp.arange(neurons, dtype=jnp.int32), perm)
    order = order.reshape(2, 2, half // 2)
    order = jnp.where(low_bit == 0, order, order[:, ::-1]).reshape(2, half)
    keep_order = jnp.where(am_target, order[0], order[1])
    send_order = jnp.where(am_target, order[1], order[0])
    columns = jnp.arange(neurons, dtype=jnp.int32)
    keep_hot = (keep_order[:, None] == columns[None, :]).astype(BF16)
    send_hot = (send_order[:, None] == columns[None, :]).astype(BF16)
    chosen = [lax.dynamic_index_in_dim(w, merged_slot, 0, keepdims=False) for w in weights]
    others = [lax.dynamic_index_in_dim(w, other_slot, 0, keepdims=False) for w in weights]
    sends = [dot(send_hot, w, 1, 1).astype(BF16) for w in chosen]
    keeps = [dot(keep_hot, w, 1, 1).astype(BF16) for w in chosen]

    inputs_x = gathered[:, :width]
    inputs_c = gathered[:, width : 2 * width]
    parts = gathered[:, 2 * width : 2 * width + 3 * experts].astype(F32)
    route_all = parts[:, :experts] + parts[:, experts : 2 * experts] + parts[:, 2 * experts :]
    merged_hit = (expert_ids == source_e) | (expert_ids == target_e)
    merged_p = jnp.sum(jnp.where(merged_hit, route_all, 0.0), axis=1)
    other_p = jnp.sum(jnp.where(expert_ids == other_e, route_all, 0.0), axis=1)
    merged_dy = (merged_p[:, None] * inputs_c.astype(F32)).astype(BF16)

    named = (other_p > 0.0).reshape(devices_n, tok_local)
    upper = jnp.arange(tok_local)[:, None] <= jnp.arange(tok_local)[None, :]
    rank = dot(named.astype(BF16), upper.astype(BF16), 1, 0).astype(jnp.int32) - 1
    block = (jnp.arange(devices_n, dtype=jnp.int32) + (1 - low_bit) * (devices_n // 2)) % devices_n
    place = jnp.where(named, block[:, None] * depth + rank, -1).reshape(tok_all)
    slot_hot = jnp.arange(slots, dtype=jnp.int32)[:, None] == place[None, :]
    slot_p = jnp.sum(jnp.where(slot_hot, other_p[None, :], 0.0), axis=1)
    slot_hot = slot_hot.astype(BF16)
    other_x = dot(slot_hot, inputs_x, 1, 0).astype(BF16)
    other_dy = (dot(slot_hot, inputs_c, 1, 0) * slot_p[:, None]).astype(BF16)

    def core_sum(send_part, keep_part):
        if hidden_n == 1:
            return keep_part.astype(BF16)
        arrived = lax.ppermute(send_part.astype(BF16), "hidden", xor_pairs(hidden_n, 1))
        return (keep_part + arrived.astype(F32)).astype(BF16)

    last_bit = 2
    while last_bit * 2 < hidden_n:
        last_bit *= 2

    def near_sum(part):
        bit = 2
        while bit < last_bit:
            arrived = lax.ppermute(part, "hidden", xor_pairs(hidden_n, bit))
            part, bit = (part.astype(F32) + arrived.astype(F32)).astype(BF16), bit * 2
        return part

    def far(part):
        if last_bit < hidden_n:
            return lax.ppermute(part, "hidden", xor_pairs(hidden_n, last_bit))
        return jnp.zeros_like(part)

    def swapped(value):
        return lax.ppermute(value, "hidden", xor_pairs(hidden_n, 1))

    slots_half = slots // 2
    quarter = half // 2

    other_parts = [
        near_sum(core_sum(dot(value[:slots_half], w, 1, 0), dot(value[slots_half:], w, 1, 0)))
        for value, w in zip((other_x, other_x, other_dy), others)
    ]

    def blend(arrived, keeps, parts):
        crossed = [far(part) for part in parts]
        merged = [elementwise(mean, 1, [pair])[0] for pair in zip(keeps, arrived)]
        return merged, crossed

    merged, other_far = with_partner(devices_n, me ^ partner, sends, blend, keeps, other_parts)
    w_down = merged[2]
    merged_sums = []
    for value, w in zip((inputs_x, inputs_x, merged_dy), merged):
        part = near_sum(core_sum(dot(w[quarter:], value, 1, 1), dot(w[:quarter], value, 1, 1)))
        merged_sums.append((part, far(part)))

    other_h, other_dg, other_du = [
        jnp.concatenate([swapped(a), a], axis=0)
        for a in elementwise(units_and_gradients, 3, list(zip(other_parts, other_far)))
    ]
    other_y = (dot(other_h, others[2], 1, 1) * slot_p[:, None]).astype(BF16)
    other_mixed = dot(slot_hot, other_y, 0, 0)
    other_grads, other_done = zip(*[
        slot_matmul(other_slot, value, a, exp_local)
        for value, a in ((other_x, other_dg), (other_x, other_du), (other_dy, other_h))
    ])

    def joined(a):
        return jnp.concatenate([a, swapped(a)], axis=0)

    (merged_h,) = elementwise(
        hidden_units,
        1,
        merged_sums[:2],
        before=(other_mixed, merged_sums[2][0], *other_done),
    )
    merged_h = joined(merged_h)
    mixed = (other_mixed + merged_p[:, None] * dot(merged_h, w_down, 0, 0)).astype(BF16)
    mixed, passed = ring_scatter(mixed, devices_n)
    merged_dg, merged_du = map(
        joined, elementwise(hidden_gradients, 2, merged_sums, before=passed[1:2])
    )
    halves = [
        dot(a, value, 1, 0).astype(BF16)
        for a, value in ((merged_dg, inputs_x), (merged_du, inputs_x), (merged_h, merged_dy))
    ]
    far_halves = with_partner(devices_n, me ^ partner, halves, list)

    keep_flag = am_target.astype(jnp.int32)
    outs = [
        slot_place(
            merged_slot,
            keep_flag,
            low_bit,
            own,
            far,
            into,
        )
        for into, own, far in zip(
            other_grads, halves, far_halves
        )
    ]
    return (mixed, *outs)


def solution(mesh):
    placed = (
        P("expert", "hidden"),
        P("expert", "hidden"),
        P("expert", "hidden", None),
        P("expert", "hidden", None),
        P("expert", "hidden", None),
        P("expert", None),
        P("expert", None),
        P(),
        P(),
        P(),
    )
    return jax.shard_map(
        shards,
        mesh=mesh,
        in_specs=placed,
        out_specs=(
            P("expert", "hidden"),
            P("expert", "hidden", None),
            P("expert", "hidden", None),
            P("expert", "hidden", None),
        ),
        check_vma=False,
    )
```

```python
import functools

import jax
import jax.numpy as jnp
from jax import lax
from jax.experimental import pallas as pl
from jax.experimental.pallas import tpu as pltpu
from jax.sharding import PartitionSpec as P

F32 = jnp.float32
BF16 = jnp.bfloat16


def dot(a, b, ca, cb):
    return lax.dot_general(a, b, (((ca,), (cb,)), ((), ())), preferred_element_type=F32)


def xor_pairs(count, bits):
    return [(i, i ^ bits) for i in range(count)]


def with_partner(count, apart, values, use, *others):
    def run(bits, values, *others):
        return use([lax.ppermute(v, "expert", xor_pairs(count, bits)) for v in values], *others)

    branches = [functools.partial(run, bits) for bits in range(1, count)]
    return lax.switch(apart - 1, branches, list(values), *others)


def never(value):
    return (value[0, 0] > 1e30).astype(jnp.int32)


def ring_gather(value, count):
    ring = [(i, (i + 2) % count) for i in range(count)]
    blocks = []
    for step in range(count // 2):
        if step > 0:
            value = lax.ppermute(value, "expert", ring)
        blocks += [value, lax.ppermute(value, "expert", xor_pairs(count, 1))]
    return jnp.concatenate(blocks, axis=0), blocks[3::2] or blocks[1:]


def ring_scatter(partial, count):
    rows = partial.shape[0] // count
    ring = [(i, (i + 2) % count) for i in range(count)]
    steps = count // 2
    twins = []
    for step in range(steps):
        at = ((step + 1) % steps * 2 + 1) * rows
        twins.append(lax.ppermute(partial[at : at + rows], "expert", xor_pairs(count, 1)))
    terms, first = [], None
    for step in range(steps):
        if step > 0:
            total = sum(term.astype(F32) for term in terms).astype(BF16)
            first = total if first is None else first
            terms = [lax.ppermute(total, "expert", ring)]
        else:
            terms = []
        at = (step + 1) % steps * 2 * rows
        terms += [partial[at : at + rows], twins[step]]
    return terms, first


def tile_of(extent, most):
    return max(t for t in range(128, most + 1, 128) if extent % t == 0)


def slot_select(slot, send_order, keep_order, weight, before):
    slots, width, neurons = weight.shape
    half = send_order.shape[0]
    tile = max(t for t in range(16, 193, 16) if half % t == 0)

    def kernel(slot_ref, send_ref, keep_ref, weight_ref, before_ref, sent_ref, kept_ref):
        columns = lax.broadcasted_iota(jnp.int32, (tile, neurons), 1)
        for order_ref, out_ref in ((send_ref, sent_ref), (keep_ref, kept_ref)):
            hot = jnp.where(order_ref[...] == columns, 1.0, 0.0).astype(BF16)
            out_ref[...] = dot(hot, weight_ref[0], 1, 1).astype(BF16)

    return pl.pallas_call(
        kernel,
        out_shape=[jax.ShapeDtypeStruct((half, width), BF16)] * 2,
        grid_spec=pltpu.PrefetchScalarGridSpec(
            num_scalar_prefetch=1,
            grid=(half // tile,),
            in_specs=[
                pl.BlockSpec((tile, 1), lambda i, s: (i, 0)),
                pl.BlockSpec((tile, 1), lambda i, s: (i, 0)),
                pl.BlockSpec((1, width, neurons), lambda i, s: (s[0], 0, 0)),
                pl.BlockSpec(memory_space=pl.ANY),
            ],
            out_specs=[pl.BlockSpec((tile, width), lambda i, s: (i, 0))] * 2,
        ),
        compiler_params=pltpu.CompilerParams(vmem_limit_bytes=32 << 20),
        cost_estimate=pl.CostEstimate(
            flops=4 * half * width * neurons,
            bytes_accessed=2 * (width * neurons + 2 * half * width),
            transcendentals=0,
        ),
    )(slot.reshape(1), send_order[:, None], keep_order[:, None], weight, before)


def slot_matmul(slot, left, right, slots):
    rows, width = left.shape
    neurons = right.shape[1]
    tile = tile_of(width, 256)

    def kernel(slot_ref, left_ref, right_ref, out_ref, done_ref):
        out_ref[0] = dot(left_ref[...], right_ref[...], 0, 0).astype(BF16)
        done_ref[...] = jnp.zeros_like(done_ref)

    return pl.pallas_call(
        kernel,
        out_shape=[
            jax.ShapeDtypeStruct((slots, width, neurons), BF16),
            jax.ShapeDtypeStruct((8, 128), F32),
        ],
        grid_spec=pltpu.PrefetchScalarGridSpec(
            num_scalar_prefetch=1,
            grid=(width // tile,),
            in_specs=[
                pl.BlockSpec((rows, tile), lambda i, s: (0, i)),
                pl.BlockSpec((rows, neurons), lambda i, s: (0, 0)),
            ],
            out_specs=[
                pl.BlockSpec((1, tile, neurons), lambda i, s: (s[0], i, 0)),
                pl.BlockSpec((8, 128), lambda i, s: (0, 0)),
            ],
        ),
        compiler_params=pltpu.CompilerParams(vmem_limit_bytes=32 << 20),
        cost_estimate=pl.CostEstimate(
            flops=2 * rows * width * neurons,
            bytes_accessed=2 * (rows * width + rows * neurons + width * neurons),
            transcendentals=0,
        ),
    )(slot.reshape(1), left, right)


def slot_place(slot, keep, swap, first, second, into):
    half, width = first.shape
    quarter = half // 2
    tile = tile_of(width, 256)

    def kernel(slot_ref, keep_ref, swap_ref, first_ref, second_ref, into_ref, out_ref):
        swap = swap_ref[0] > 0
        parts = []
        for ref in (first_ref, second_ref):
            one, two = ref[:quarter], ref[quarter:]
            parts += [jnp.where(swap, two, one), jnp.where(swap, one, two)]
        whole = jnp.concatenate(parts, axis=0)
        whole = jnp.where(keep_ref[0] > 0, whole, jnp.zeros((), BF16))
        out_ref[0] = whole.T

    return pl.pallas_call(
        kernel,
        out_shape=jax.ShapeDtypeStruct(into.shape, BF16),
        grid_spec=pltpu.PrefetchScalarGridSpec(
            num_scalar_prefetch=3,
            grid=(width // tile,),
            in_specs=[
                pl.BlockSpec((half, tile), lambda i, s, k, w: (0, i)),
                pl.BlockSpec((half, tile), lambda i, s, k, w: (0, i)),
                pl.BlockSpec(memory_space=pl.ANY),
            ],
            out_specs=pl.BlockSpec((1, tile, 2 * half), lambda i, s, k, w: (s[0], i, 0)),
        ),
        input_output_aliases={5: 0},
        compiler_params=pltpu.CompilerParams(vmem_limit_bytes=32 << 20),
        cost_estimate=pl.CostEstimate(
            flops=0, bytes_accessed=8 * half * width, transcendentals=0
        ),
    )(slot.reshape(1), keep.reshape(1), swap.reshape(1), first, second, into)


def mean(total):
    return (0.5 * total,)


def hidden_units(gate_sum, up_sum):
    return (gate_sum * jax.nn.sigmoid(gate_sum) * up_sum,)


def hidden_gradients(gate_sum, up_sum, back_sum):
    sigma = jax.nn.sigmoid(gate_sum)
    slope = sigma * (1.0 + gate_sum * (1.0 - sigma))
    return back_sum * up_sum * slope, back_sum * (gate_sum * sigma)


def units_and_gradients(*sums):
    return *hidden_units(*sums[:2]), *hidden_gradients(*sums)


def elementwise(function, count, pairs, before=()):
    rows, cols = pairs[0][0].shape
    tile = max(t for t in range(16, 193, 16) if rows % t == 0)
    values = [value for pair in pairs for value in pair]

    def kernel(*refs):
        outs = refs[len(values) + len(before) :]

        def strip(i, carry):
            at = pl.ds(pl.multiple_of(i * 16, 16), 16)
            sums = [
                refs[2 * j][at, :].astype(F32) + refs[2 * j + 1][at, :].astype(F32)
                for j in range(len(pairs))
            ]
            for ref, result in zip(outs, function(*sums)):
                ref[at, :] = result.astype(BF16)
            return carry

        lax.fori_loop(0, tile // 16, strip, 0)

    spec = pl.BlockSpec((tile, cols), lambda i: (i, 0))
    return pl.pallas_call(
        kernel,
        out_shape=[jax.ShapeDtypeStruct((rows, cols), BF16)] * count,
        grid=(rows // tile,),
        in_specs=[spec] * len(values) + [pl.BlockSpec(memory_space=pl.ANY)] * len(before),
        out_specs=[spec] * count,
        compiler_params=pltpu.CompilerParams(vmem_limit_bytes=32 << 20),
        cost_estimate=pl.CostEstimate(
            flops=20 * rows * cols,
            bytes_accessed=2 * rows * cols * (len(values) + count),
            transcendentals=rows * cols,
        ),
    )(*values, *before)


def shards(
    tokens,
    cotangent,
    gate_weight,
    up_weight,
    down_weight,
    routing,
    route_weight,
    merge_source,
    merge_target,
    neuron_perm,
):
    devices_n = lax.axis_size("expert")
    hidden_n = lax.axis_size("hidden")
    me = lax.axis_index("expert")
    low_bit = lax.axis_index("hidden") % 2
    exp_local, width, neurons = gate_weight.shape
    experts = exp_local * devices_n
    tok_local, top_count = routing.shape
    tok_all = tok_local * devices_n
    depth = max(2, tok_local * top_count * 4 // (3 * experts))
    slots = devices_n * depth
    half = neurons // 2
    weights = (gate_weight, up_weight, down_weight)

    expert_ids = jnp.arange(experts, dtype=jnp.int32)
    route = jnp.sum(
        jnp.where(routing[:, :, None] == expert_ids, route_weight[:, :, None], 0.0), axis=1
    )
    high = lax.reduce_precision(route, 8, 7)
    middle = lax.reduce_precision(route - high, 8, 7)
    low = route - high - middle
    pieces = jnp.concatenate([high, middle, low], axis=1).astype(BF16)
    pad = -pieces.shape[1] % 128
    payload = jnp.concatenate([tokens, cotangent, jnp.pad(pieces, ((0, 0), (0, pad)))], axis=1)
    gathered, twins = ring_gather(payload, devices_n)

    source_dev = merge_source // exp_local
    target_dev = merge_target // exp_local
    is_source = source_dev == me
    is_target = target_dev == me
    mine = is_source | is_target
    am_target = jnp.any(is_target)
    partner = jnp.sum(jnp.where(is_source, target_dev, 0) + jnp.where(is_target, source_dev, 0))
    source_e = jnp.sum(jnp.where(mine, merge_source, 0))
    target_e = jnp.sum(jnp.where(mine, merge_target, 0))
    merged_slot = jnp.where(am_target, target_e, source_e) % exp_local
    other_slot = exp_local - 1 - merged_slot
    other_e = me * exp_local + other_slot
    perm = jnp.sum(jnp.where(mine[:, None], neuron_perm, 0), axis=0)

    order = jnp.where(am_target, jnp.arange(neurons, dtype=jnp.int32), perm)
    order = order.reshape(2, 2, half // 2)
    order = jnp.where(low_bit == 0, order, order[:, ::-1]).reshape(2, half)
    keep_order = jnp.where(am_target, order[0], order[1])
    send_order = jnp.where(am_target, order[1], order[0])
    sends, keeps = zip(*[
        slot_select(merged_slot, send_order, keep_order, w, twins[min(i, len(twins) - 1)])
        for i, w in enumerate(weights)
    ])
    others = [lax.dynamic_index_in_dim(w, other_slot, 0, keepdims=False) for w in weights]

    inputs_x = gathered[:, :width]
    inputs_c = gathered[:, width : 2 * width]
    parts = gathered[:, 2 * width : 2 * width + 3 * experts].astype(F32)
    route_all = parts[:, :experts] + parts[:, experts : 2 * experts] + parts[:, 2 * experts :]
    merged_hit = (expert_ids == source_e) | (expert_ids == target_e)
    merged_p = jnp.sum(jnp.where(merged_hit, route_all, 0.0), axis=1)
    other_p = jnp.sum(jnp.where(expert_ids == other_e, route_all, 0.0), axis=1)
    merged_dy = (merged_p[:, None] * inputs_c.astype(F32)).astype(BF16)

    named = (other_p > 0.0).reshape(devices_n, tok_local)
    upper = jnp.arange(tok_local)[:, None] <= jnp.arange(tok_local)[None, :]
    rank = dot(named.astype(BF16), upper.astype(BF16), 1, 0).astype(jnp.int32) - 1
    block = (jnp.arange(devices_n, dtype=jnp.int32) + (1 - low_bit) * (devices_n // 2)) % devices_n
    place = jnp.where(named, block[:, None] * depth + rank, -1).reshape(tok_all)
    slot_hot = jnp.arange(slots, dtype=jnp.int32)[:, None] == place[None, :]
    slot_p = jnp.sum(jnp.where(slot_hot, other_p[None, :], 0.0), axis=1)
    slot_hot = slot_hot.astype(BF16)
    other_x = dot(slot_hot, inputs_x, 1, 0).astype(BF16)
    other_dy = (dot(slot_hot, inputs_c, 1, 0) * slot_p[:, None]).astype(BF16)

    def core_sum(send_part, keep_part):
        if hidden_n == 1:
            return keep_part.astype(BF16)
        arrived = lax.ppermute(send_part.astype(BF16), "hidden", xor_pairs(hidden_n, 1))
        return (keep_part + arrived.astype(F32)).astype(BF16)

    last_bit = 2
    while last_bit * 2 < hidden_n:
        last_bit *= 2

    def near_sum(part):
        bit = 2
        while bit < last_bit:
            arrived = lax.ppermute(part, "hidden", xor_pairs(hidden_n, bit))
            part, bit = (part.astype(F32) + arrived.astype(F32)).astype(BF16), bit * 2
        return part

    def far(part):
        if last_bit < hidden_n:
            return lax.ppermute(part, "hidden", xor_pairs(hidden_n, last_bit))
        return jnp.zeros_like(part)

    def swapped(value):
        return lax.ppermute(value, "hidden", xor_pairs(hidden_n, 1))

    slots_half = slots // 2
    quarter = half // 2

    other_parts = [
        near_sum(core_sum(dot(value[:slots_half], w, 1, 0), dot(value[slots_half:], w, 1, 0)))
        for value, w in zip((other_x, other_x, other_dy), others)
    ]

    def blend(arrived, keeps, parts):
        crossed = [far(part) for part in parts]
        merged = [elementwise(mean, 1, [pair])[0] for pair in zip(keeps, arrived)]
        return merged, crossed

    merged, other_far = with_partner(devices_n, me ^ partner, sends, blend, keeps, other_parts)
    w_down = merged[2]
    merged_sums = []
    for value, w in zip((inputs_x, inputs_x, merged_dy), merged):
        part = near_sum(core_sum(dot(w[quarter:], value, 1, 1), dot(w[:quarter], value, 1, 1)))
        merged_sums.append((part, far(part)))

    other_h, other_dg, other_du = [
        jnp.concatenate([swapped(a), a], axis=0)
        for a in elementwise(units_and_gradients, 3, list(zip(other_parts, other_far)))
    ]
    other_y = (dot(other_h, others[2], 1, 1) * slot_p[:, None]).astype(BF16)
    other_mixed = dot(slot_hot, other_y, 0, 0)
    other_grads, other_done = zip(*[
        slot_matmul(other_slot, value, a, exp_local)
        for value, a in ((other_x, other_dg), (other_x, other_du), (other_dy, other_h))
    ])

    def joined(a):
        return jnp.concatenate([a, swapped(a)], axis=0)

    (merged_h,) = elementwise(
        hidden_units,
        1,
        merged_sums[:2],
        before=(other_mixed, merged_sums[2][0], *other_done),
    )
    merged_h = joined(merged_h)
    mixed = (other_mixed + merged_p[:, None] * dot(merged_h, w_down, 0, 0)).astype(BF16)
    mixed_terms, first_sum = ring_scatter(mixed, devices_n)
    merged_dg, merged_du = map(
        joined, elementwise(hidden_gradients, 2, merged_sums, before=(first_sum,))
    )
    halves = [
        dot(a, value, 1, 0).astype(BF16)
        for a, value in ((merged_dg, inputs_x), (merged_du, inputs_x), (merged_h, merged_dy))
    ]
    far_halves = with_partner(devices_n, me ^ partner, halves, list)

    mixed = sum((t.astype(F32) for t in mixed_terms), never(far_halves[0]).astype(F32))
    mixed = mixed.astype(BF16)

    keep_flag = am_target.astype(jnp.int32)
    outs = [
        slot_place(
            merged_slot,
            keep_flag,
            low_bit,
            own,
            far,
            into,
        )
        for into, own, far in zip(
            other_grads, halves, far_halves
        )
    ]
    return (mixed, *outs)


def solution(mesh):
    placed = (
        P("expert", "hidden"),
        P("expert", "hidden"),
        P("expert", "hidden", None),
        P("expert", "hidden", None),
        P("expert", "hidden", None),
        P("expert", None),
        P("expert", None),
        P(),
        P(),
        P(),
    )
    return jax.shard_map(
        shards,
        mesh=mesh,
        in_specs=placed,
        out_specs=(
            P("expert", "hidden"),
            P("expert", "hidden", None),
            P("expert", "hidden", None),
            P("expert", "hidden", None),
        ),
        check_vma=False,
    )
```

```python
import functools

import jax
import jax.numpy as jnp
from jax import lax
from jax.experimental import pallas as pl
from jax.experimental.pallas import tpu as pltpu
from jax.sharding import PartitionSpec as P

F32 = jnp.float32
BF16 = jnp.bfloat16


def dot(a, b, ca, cb):
    return lax.dot_general(a, b, (((ca,), (cb,)), ((), ())), preferred_element_type=F32)


def xor_pairs(count, bits):
    return [(i, i ^ bits) for i in range(count)]


def with_partner(count, apart, values, use, *others):
    def run(bits, values, *others):
        return use([lax.ppermute(v, "expert", xor_pairs(count, bits)) for v in values], *others)

    branches = [functools.partial(run, bits) for bits in range(1, count)]
    return lax.switch(apart - 1, branches, list(values), *others)


def never(value):
    return (value[0, 0] > 1e30).astype(jnp.int32)


def ring_gather(value, count):
    ring = [(i, (i + 2) % count) for i in range(count)]
    blocks = []
    for step in range(count // 2):
        if step > 0:
            value = lax.ppermute(value, "expert", ring)
        blocks += [value, lax.ppermute(value, "expert", xor_pairs(count, 1))]
    return jnp.concatenate(blocks, axis=0), blocks[3::2] or blocks[1:]


def ring_scatter(partial, count):
    rows = partial.shape[0] // count
    ring = [(i, (i + 2) % count) for i in range(count)]
    steps = count // 2
    twins = []
    for step in range(steps):
        at = ((step + 1) % steps * 2 + 1) * rows
        twins.append(lax.ppermute(partial[at : at + rows], "expert", xor_pairs(count, 1)))
    owns = []
    for step in range(steps):
        at = (step + 1) % steps * 2 * rows
        owns.append((partial[at : at + rows], twins[step]))

    def added(*terms):
        return sum(term.astype(F32) for term in terms)

    def hop(total):
        return lax.ppermute(total, "expert", ring)

    total = added(*owns[0]).astype(BF16)
    held = max(1, steps - 2)
    for own in owns[1:held]:
        total = added(*own, hop(total)).astype(BF16)
    arrived = [hop(total)] if steps > 1 else []

    def end(later):
        if steps == 1:
            return total
        result = added(*owns[held], *arrived, never(later))
        for own in owns[held + 1 :]:
            result = added(*own, hop(result.astype(BF16)))
        return result.astype(BF16)

    return end, total


def tile_of(extent, most):
    return max(t for t in range(128, most + 1, 128) if extent % t == 0)


def slot_select(slot, send_order, keep_order, weight, before):
    slots, width, neurons = weight.shape
    half = send_order.shape[0]
    tile = max(t for t in range(16, 353, 16) if half % t == 0)

    def kernel(slot_ref, send_ref, keep_ref, weight_ref, before_ref, sent_ref, kept_ref):
        columns = lax.broadcasted_iota(jnp.int32, (tile, neurons), 1)
        for order_ref, out_ref in ((send_ref, sent_ref), (keep_ref, kept_ref)):
            hot = jnp.where(order_ref[...] == columns, 1.0, 0.0).astype(BF16)
            out_ref[...] = dot(hot, weight_ref[0], 1, 1).astype(BF16)

    return pl.pallas_call(
        kernel,
        out_shape=[jax.ShapeDtypeStruct((half, width), BF16)] * 2,
        grid_spec=pltpu.PrefetchScalarGridSpec(
            num_scalar_prefetch=1,
            grid=(half // tile,),
            in_specs=[
                pl.BlockSpec((tile, 1), lambda i, s: (i, 0)),
                pl.BlockSpec((tile, 1), lambda i, s: (i, 0)),
                pl.BlockSpec((1, width, neurons), lambda i, s: (s[0], 0, 0)),
                pl.BlockSpec(memory_space=pl.ANY),
            ],
            out_specs=[pl.BlockSpec((tile, width), lambda i, s: (i, 0))] * 2,
        ),
        compiler_params=pltpu.CompilerParams(vmem_limit_bytes=32 << 20),
        cost_estimate=pl.CostEstimate(
            flops=4 * half * width * neurons,
            bytes_accessed=2 * (width * neurons + 2 * half * width),
            transcendentals=0,
        ),
    )(slot.reshape(1), send_order[:, None], keep_order[:, None], weight, before)


def slot_matmul(slot, left, right, slots):
    rows, width = left.shape
    neurons = right.shape[1]
    tile = tile_of(width, 256)

    def kernel(slot_ref, left_ref, right_ref, out_ref, done_ref):
        out_ref[0] = dot(left_ref[...], right_ref[...], 0, 0).astype(BF16)
        done_ref[...] = jnp.zeros_like(done_ref)

    return pl.pallas_call(
        kernel,
        out_shape=[
            jax.ShapeDtypeStruct((slots, width, neurons), BF16),
            jax.ShapeDtypeStruct((8, 128), F32),
        ],
        grid_spec=pltpu.PrefetchScalarGridSpec(
            num_scalar_prefetch=1,
            grid=(width // tile,),
            in_specs=[
                pl.BlockSpec((rows, tile), lambda i, s: (0, i)),
                pl.BlockSpec((rows, neurons), lambda i, s: (0, 0)),
            ],
            out_specs=[
                pl.BlockSpec((1, tile, neurons), lambda i, s: (s[0], i, 0)),
                pl.BlockSpec((8, 128), lambda i, s: (0, 0)),
            ],
        ),
        compiler_params=pltpu.CompilerParams(vmem_limit_bytes=32 << 20),
        cost_estimate=pl.CostEstimate(
            flops=2 * rows * width * neurons,
            bytes_accessed=2 * (rows * width + rows * neurons + width * neurons),
            transcendentals=0,
        ),
    )(slot.reshape(1), left, right)


def slot_place(slot, keep, swap, first, second, into):
    half, width = first.shape
    quarter = half // 2
    tile = tile_of(width, 256)

    def kernel(slot_ref, keep_ref, swap_ref, first_ref, second_ref, into_ref, out_ref):
        swap = swap_ref[0] > 0
        parts = []
        for ref in (first_ref, second_ref):
            one, two = ref[:quarter], ref[quarter:]
            parts += [jnp.where(swap, two, one), jnp.where(swap, one, two)]
        whole = jnp.concatenate(parts, axis=0)
        whole = jnp.where(keep_ref[0] > 0, whole, jnp.zeros((), BF16))
        out_ref[0] = whole.T

    return pl.pallas_call(
        kernel,
        out_shape=jax.ShapeDtypeStruct(into.shape, BF16),
        grid_spec=pltpu.PrefetchScalarGridSpec(
            num_scalar_prefetch=3,
            grid=(width // tile,),
            in_specs=[
                pl.BlockSpec((half, tile), lambda i, s, k, w: (0, i)),
                pl.BlockSpec((half, tile), lambda i, s, k, w: (0, i)),
                pl.BlockSpec(memory_space=pl.ANY),
            ],
            out_specs=pl.BlockSpec((1, tile, 2 * half), lambda i, s, k, w: (s[0], i, 0)),
        ),
        input_output_aliases={5: 0},
        compiler_params=pltpu.CompilerParams(vmem_limit_bytes=32 << 20),
        cost_estimate=pl.CostEstimate(
            flops=0, bytes_accessed=8 * half * width, transcendentals=0
        ),
    )(slot.reshape(1), keep.reshape(1), swap.reshape(1), first, second, into)


def mean(total):
    return (0.5 * total,)


def hidden_units(gate_sum, up_sum):
    return (gate_sum * jax.nn.sigmoid(gate_sum) * up_sum,)


def hidden_gradients(gate_sum, up_sum, back_sum):
    sigma = jax.nn.sigmoid(gate_sum)
    slope = sigma * (1.0 + gate_sum * (1.0 - sigma))
    return back_sum * up_sum * slope, back_sum * (gate_sum * sigma)


def units_and_gradients(*sums):
    return *hidden_units(*sums[:2]), *hidden_gradients(*sums)


def elementwise(function, count, pairs, before=()):
    rows, cols = pairs[0][0].shape
    tile = max(t for t in range(16, 193, 16) if rows % t == 0)
    values = [value for pair in pairs for value in pair]

    def kernel(*refs):
        outs = refs[len(values) + len(before) :]

        def strip(i, carry):
            at = pl.ds(pl.multiple_of(i * 16, 16), 16)
            sums = [
                refs[2 * j][at, :].astype(F32) + refs[2 * j + 1][at, :].astype(F32)
                for j in range(len(pairs))
            ]
            for ref, result in zip(outs, function(*sums)):
                ref[at, :] = result.astype(BF16)
            return carry

        lax.fori_loop(0, tile // 16, strip, 0)

    spec = pl.BlockSpec((tile, cols), lambda i: (i, 0))
    return pl.pallas_call(
        kernel,
        out_shape=[jax.ShapeDtypeStruct((rows, cols), BF16)] * count,
        grid=(rows // tile,),
        in_specs=[spec] * len(values) + [pl.BlockSpec(memory_space=pl.ANY)] * len(before),
        out_specs=[spec] * count,
        compiler_params=pltpu.CompilerParams(vmem_limit_bytes=32 << 20),
        cost_estimate=pl.CostEstimate(
            flops=20 * rows * cols,
            bytes_accessed=2 * rows * cols * (len(values) + count),
            transcendentals=rows * cols,
        ),
    )(*values, *before)


def shards(
    tokens,
    cotangent,
    gate_weight,
    up_weight,
    down_weight,
    routing,
    route_weight,
    merge_source,
    merge_target,
    neuron_perm,
):
    devices_n = lax.axis_size("expert")
    hidden_n = lax.axis_size("hidden")
    me = lax.axis_index("expert")
    low_bit = lax.axis_index("hidden") % 2
    exp_local, width, neurons = gate_weight.shape
    experts = exp_local * devices_n
    tok_local, top_count = routing.shape
    tok_all = tok_local * devices_n
    depth = max(2, tok_local * top_count * 4 // (3 * experts))
    slots = devices_n * depth
    half = neurons // 2
    weights = (gate_weight, up_weight, down_weight)

    expert_ids = jnp.arange(experts, dtype=jnp.int32)
    route = jnp.sum(
        jnp.where(routing[:, :, None] == expert_ids, route_weight[:, :, None], 0.0), axis=1
    )
    high = lax.reduce_precision(route, 8, 7)
    middle = lax.reduce_precision(route - high, 8, 7)
    low = route - high - middle
    pieces = jnp.concatenate([high, middle, low], axis=1).astype(BF16)
    pad = -pieces.shape[1] % 128
    payload = jnp.concatenate([tokens, cotangent, jnp.pad(pieces, ((0, 0), (0, pad)))], axis=1)
    gathered, twins = ring_gather(payload, devices_n)

    source_dev = merge_source // exp_local
    target_dev = merge_target // exp_local
    is_source = source_dev == me
    is_target = target_dev == me
    mine = is_source | is_target
    am_target = jnp.any(is_target)
    partner = jnp.sum(jnp.where(is_source, target_dev, 0) + jnp.where(is_target, source_dev, 0))
    source_e = jnp.sum(jnp.where(mine, merge_source, 0))
    target_e = jnp.sum(jnp.where(mine, merge_target, 0))
    merged_slot = jnp.where(am_target, target_e, source_e) % exp_local
    other_slot = exp_local - 1 - merged_slot
    other_e = me * exp_local + other_slot
    perm = jnp.sum(jnp.where(mine[:, None], neuron_perm, 0), axis=0)

    order = jnp.where(am_target, jnp.arange(neurons, dtype=jnp.int32), perm)
    order = order.reshape(2, 2, half // 2)
    order = jnp.where(low_bit == 0, order, order[:, ::-1]).reshape(2, half)
    keep_order = jnp.where(am_target, order[0], order[1])
    send_order = jnp.where(am_target, order[1], order[0])
    sends, keeps = zip(*[
        slot_select(merged_slot, send_order, keep_order, w, twins[min(i, len(twins) - 1)])
        for i, w in enumerate(weights)
    ])
    others = [lax.dynamic_index_in_dim(w, other_slot, 0, keepdims=False) for w in weights]

    inputs_x = gathered[:, :width]
    inputs_c = gathered[:, width : 2 * width]
    parts = gathered[:, 2 * width : 2 * width + 3 * experts].astype(F32)
    route_all = parts[:, :experts] + parts[:, experts : 2 * experts] + parts[:, 2 * experts :]
    merged_hit = (expert_ids == source_e) | (expert_ids == target_e)
    merged_p = jnp.sum(jnp.where(merged_hit, route_all, 0.0), axis=1)
    other_p = jnp.sum(jnp.where(expert_ids == other_e, route_all, 0.0), axis=1)
    merged_dy = (merged_p[:, None] * inputs_c.astype(F32)).astype(BF16)

    named = (other_p > 0.0).reshape(devices_n, tok_local)
    upper = jnp.arange(tok_local)[:, None] <= jnp.arange(tok_local)[None, :]
    rank = dot(named.astype(BF16), upper.astype(BF16), 1, 0).astype(jnp.int32) - 1
    block = (jnp.arange(devices_n, dtype=jnp.int32) + (1 - low_bit) * (devices_n // 2)) % devices_n
    place = jnp.where(named, block[:, None] * depth + rank, -1).reshape(tok_all)
    slot_hot = jnp.arange(slots, dtype=jnp.int32)[:, None] == place[None, :]
    slot_p = jnp.sum(jnp.where(slot_hot, other_p[None, :], 0.0), axis=1)
    slot_hot = slot_hot.astype(BF16)
    other_x = dot(slot_hot, inputs_x, 1, 0).astype(BF16)
    other_dy = (dot(slot_hot, inputs_c, 1, 0) * slot_p[:, None]).astype(BF16)

    def core_sum(send_part, keep_part):
        if hidden_n == 1:
            return keep_part.astype(BF16)
        arrived = lax.ppermute(send_part.astype(BF16), "hidden", xor_pairs(hidden_n, 1))
        return (keep_part + arrived.astype(F32)).astype(BF16)

    last_bit = 2
    while last_bit * 2 < hidden_n:
        last_bit *= 2

    def near_sum(part):
        bit = 2
        while bit < last_bit:
            arrived = lax.ppermute(part, "hidden", xor_pairs(hidden_n, bit))
            part, bit = (part.astype(F32) + arrived.astype(F32)).astype(BF16), bit * 2
        return part

    def far(part):
        if last_bit < hidden_n:
            return lax.ppermute(part, "hidden", xor_pairs(hidden_n, last_bit))
        return jnp.zeros_like(part)

    def swapped(value):
        return lax.ppermute(value, "hidden", xor_pairs(hidden_n, 1))

    slots_half = slots // 2
    quarter = half // 2

    other_parts = [
        near_sum(core_sum(dot(value[:slots_half], w, 1, 0), dot(value[slots_half:], w, 1, 0)))
        for value, w in zip((other_x, other_x, other_dy), others)
    ]

    def blend(arrived, keeps, parts):
        crossed = [far(part) for part in parts]
        merged = [elementwise(mean, 1, [pair])[0] for pair in zip(keeps, arrived)]
        return merged, crossed

    merged, other_far = with_partner(devices_n, me ^ partner, sends, blend, keeps, other_parts)
    w_down = merged[2]
    merged_sums = []
    for value, w in zip((inputs_x, inputs_x, merged_dy), merged):
        part = near_sum(core_sum(dot(w[quarter:], value, 1, 1), dot(w[:quarter], value, 1, 1)))
        merged_sums.append((part, far(part)))

    other_h, other_dg, other_du = [
        jnp.concatenate([swapped(a), a], axis=0)
        for a in elementwise(units_and_gradients, 3, list(zip(other_parts, other_far)))
    ]
    other_y = (dot(other_h, others[2], 1, 1) * slot_p[:, None]).astype(BF16)
    other_mixed = dot(slot_hot, other_y, 0, 0)
    other_grads, other_done = zip(*[
        slot_matmul(other_slot, value, a, exp_local)
        for value, a in ((other_x, other_dg), (other_x, other_du), (other_dy, other_h))
    ])

    def joined(a):
        return jnp.concatenate([a, swapped(a)], axis=0)

    (merged_h,) = elementwise(
        hidden_units,
        1,
        merged_sums[:2],
        before=(other_mixed[:8, :128], merged_sums[2][0], *other_done),
    )
    merged_h = joined(merged_h)
    mixed = (other_mixed + merged_p[:, None] * dot(merged_h, w_down, 0, 0)).astype(BF16)
    end_ring, passed = ring_scatter(mixed, devices_n)
    merged_dg, merged_du = map(
        joined, elementwise(hidden_gradients, 2, merged_sums, before=(passed,))
    )
    halves = [
        dot(a, value, 1, 0).astype(BF16)
        for a, value in ((merged_dg, inputs_x), (merged_du, inputs_x), (merged_h, merged_dy))
    ]
    far_halves = with_partner(devices_n, me ^ partner, halves, list)

    mixed = end_ring(far_halves[0])

    keep_flag = am_target.astype(jnp.int32)
    outs = [
        slot_place(
            merged_slot,
            keep_flag,
            low_bit,
            own,
            far,
            into,
        )
        for into, own, far in zip(
            other_grads, halves, far_halves
        )
    ]
    return (mixed, *outs)


def solution(mesh):
    placed = (
        P("expert", "hidden"),
        P("expert", "hidden"),
        P("expert", "hidden", None),
        P("expert", "hidden", None),
        P("expert", "hidden", None),
        P("expert", None),
        P("expert", None),
        P(),
        P(),
        P(),
    )
    return jax.shard_map(
        shards,
        mesh=mesh,
        in_specs=placed,
        out_specs=(
            P("expert", "hidden"),
            P("expert", "hidden", None),
            P("expert", "hidden", None),
            P("expert", "hidden", None),
        ),
        check_vma=False,
    )
```

```python
import functools

import jax
import jax.numpy as jnp
from jax import lax
from jax.experimental import pallas as pl
from jax.experimental.pallas import tpu as pltpu
from jax.sharding import PartitionSpec as P

F32 = jnp.float32
BF16 = jnp.bfloat16


def dot(a, b, ca, cb):
    return lax.dot_general(a, b, (((ca,), (cb,)), ((), ())), preferred_element_type=F32)


def xor_pairs(count, bits):
    return [(i, i ^ bits) for i in range(count)]


def with_partner(count, apart, values, use, *others):
    def run(bits, values, *others):
        return use([lax.ppermute(v, "expert", xor_pairs(count, bits)) for v in values], *others)

    branches = [functools.partial(run, bits) for bits in range(1, count)]
    return lax.switch(apart - 1, branches, list(values), *others)


def never(value):
    return (value[0, 0] > 1e30).astype(jnp.int32)


def ring_gather(value, count):
    ring = [(i, (i + 2) % count) for i in range(count)]
    blocks = []
    for step in range(count // 2):
        if step > 0:
            value = lax.ppermute(value, "expert", ring)
        blocks += [value, lax.ppermute(value, "expert", xor_pairs(count, 1))]
    return jnp.concatenate(blocks, axis=0), blocks[3::2] or blocks[1:]


def ring_scatter(partial, count, later):
    rows = partial.shape[0] // count
    ring = [(i, (i + 2) % count) for i in range(count)]
    steps = count // 2
    twins = []
    for step in range(steps):
        at = ((step + 1) % steps * 2 + 1) * rows
        twins.append(lax.ppermute(partial[at : at + rows], "expert", xor_pairs(count, 1)))
    owns = []
    for step in range(steps):
        at = (step + 1) % steps * 2 * rows
        owns.append((partial[at : at + rows], twins[step]))

    def added(*terms):
        return sum(term.astype(F32) for term in terms)

    def hop(total):
        return lax.ppermute(total, "expert", ring)

    total = added(*owns[0])
    for step in range(1, steps):
        total = added(*owns[step], hop(total.astype(BF16)))
        if step == max(1, steps - 2):
            total = total + never(later)
    return total.astype(BF16)


def tile_of(extent, most):
    return max(t for t in range(128, most + 1, 128) if extent % t == 0)


def slot_select(slot, send_order, keep_order, weight, before):
    slots, width, neurons = weight.shape
    half = send_order.shape[0]
    tile = max(t for t in range(16, 353, 16) if half % t == 0)

    def kernel(slot_ref, send_ref, keep_ref, weight_ref, before_ref, sent_ref, kept_ref):
        columns = lax.broadcasted_iota(jnp.int32, (tile, neurons), 1)
        for order_ref, out_ref in ((send_ref, sent_ref), (keep_ref, kept_ref)):
            hot = jnp.where(order_ref[...] == columns, 1.0, 0.0).astype(BF16)
            out_ref[...] = dot(hot, weight_ref[0], 1, 1).astype(BF16)

    return pl.pallas_call(
        kernel,
        out_shape=[jax.ShapeDtypeStruct((half, width), BF16)] * 2,
        grid_spec=pltpu.PrefetchScalarGridSpec(
            num_scalar_prefetch=1,
            grid=(half // tile,),
            in_specs=[
                pl.BlockSpec((tile, 1), lambda i, s: (i, 0)),
                pl.BlockSpec((tile, 1), lambda i, s: (i, 0)),
                pl.BlockSpec((1, width, neurons), lambda i, s: (s[0], 0, 0)),
                pl.BlockSpec(memory_space=pl.ANY),
            ],
            out_specs=[pl.BlockSpec((tile, width), lambda i, s: (i, 0))] * 2,
        ),
        compiler_params=pltpu.CompilerParams(vmem_limit_bytes=32 << 20),
        cost_estimate=pl.CostEstimate(
            flops=4 * half * width * neurons,
            bytes_accessed=2 * (width * neurons + 2 * half * width),
            transcendentals=0,
        ),
    )(slot.reshape(1), send_order[:, None], keep_order[:, None], weight, before)


def slot_matmul(slot, left, right, slots):
    rows, width = left.shape
    neurons = right.shape[1]
    tile = tile_of(width, 256)

    def kernel(slot_ref, left_ref, right_ref, out_ref, done_ref):
        out_ref[0] = dot(left_ref[...], right_ref[...], 0, 0).astype(BF16)
        done_ref[...] = jnp.zeros_like(done_ref)

    return pl.pallas_call(
        kernel,
        out_shape=[
            jax.ShapeDtypeStruct((slots, width, neurons), BF16),
            jax.ShapeDtypeStruct((8, 128), F32),
        ],
        grid_spec=pltpu.PrefetchScalarGridSpec(
            num_scalar_prefetch=1,
            grid=(width // tile,),
            in_specs=[
                pl.BlockSpec((rows, tile), lambda i, s: (0, i)),
                pl.BlockSpec((rows, neurons), lambda i, s: (0, 0)),
            ],
            out_specs=[
                pl.BlockSpec((1, tile, neurons), lambda i, s: (s[0], i, 0)),
                pl.BlockSpec((8, 128), lambda i, s: (0, 0)),
            ],
        ),
        compiler_params=pltpu.CompilerParams(vmem_limit_bytes=32 << 20),
        cost_estimate=pl.CostEstimate(
            flops=2 * rows * width * neurons,
            bytes_accessed=2 * (rows * width + rows * neurons + width * neurons),
            transcendentals=0,
        ),
    )(slot.reshape(1), left, right)


def slot_place(slot, keep, swap, first, second, into):
    half, width = first.shape
    quarter = half // 2
    tile = tile_of(width, 256)

    def kernel(slot_ref, keep_ref, swap_ref, first_ref, second_ref, into_ref, out_ref):
        swap = swap_ref[0] > 0
        parts = []
        for ref in (first_ref, second_ref):
            one, two = ref[:quarter], ref[quarter:]
            parts += [jnp.where(swap, two, one), jnp.where(swap, one, two)]
        whole = jnp.concatenate(parts, axis=0)
        whole = jnp.where(keep_ref[0] > 0, whole, jnp.zeros((), BF16))
        out_ref[0] = whole.T

    return pl.pallas_call(
        kernel,
        out_shape=jax.ShapeDtypeStruct(into.shape, BF16),
        grid_spec=pltpu.PrefetchScalarGridSpec(
            num_scalar_prefetch=3,
            grid=(width // tile,),
            in_specs=[
                pl.BlockSpec((half, tile), lambda i, s, k, w: (0, i)),
                pl.BlockSpec((half, tile), lambda i, s, k, w: (0, i)),
                pl.BlockSpec(memory_space=pl.ANY),
            ],
            out_specs=pl.BlockSpec((1, tile, 2 * half), lambda i, s, k, w: (s[0], i, 0)),
        ),
        input_output_aliases={5: 0},
        compiler_params=pltpu.CompilerParams(vmem_limit_bytes=32 << 20),
        cost_estimate=pl.CostEstimate(
            flops=0, bytes_accessed=8 * half * width, transcendentals=0
        ),
    )(slot.reshape(1), keep.reshape(1), swap.reshape(1), first, second, into)


def mean(total):
    return (0.5 * total,)


def hidden_units(gate_sum, up_sum):
    return (gate_sum * jax.nn.sigmoid(gate_sum) * up_sum,)


def hidden_gradients(gate_sum, up_sum, back_sum):
    sigma = jax.nn.sigmoid(gate_sum)
    slope = sigma * (1.0 + gate_sum * (1.0 - sigma))
    return back_sum * up_sum * slope, back_sum * (gate_sum * sigma)


def units_and_gradients(*sums):
    return *hidden_units(*sums[:2]), *hidden_gradients(*sums)


def elementwise(function, count, pairs, before=()):
    rows, cols = pairs[0][0].shape
    tile = max(t for t in range(16, 193, 16) if rows % t == 0)
    values = [value for pair in pairs for value in pair]

    def kernel(*refs):
        outs = refs[len(values) + len(before) :]

        def strip(i, carry):
            at = pl.ds(pl.multiple_of(i * 16, 16), 16)
            sums = [
                refs[2 * j][at, :].astype(F32) + refs[2 * j + 1][at, :].astype(F32)
                for j in range(len(pairs))
            ]
            for ref, result in zip(outs, function(*sums)):
                ref[at, :] = result.astype(BF16)
            return carry

        lax.fori_loop(0, tile // 16, strip, 0)

    spec = pl.BlockSpec((tile, cols), lambda i: (i, 0))
    return pl.pallas_call(
        kernel,
        out_shape=[jax.ShapeDtypeStruct((rows, cols), BF16)] * count,
        grid=(rows // tile,),
        in_specs=[spec] * len(values) + [pl.BlockSpec(memory_space=pl.ANY)] * len(before),
        out_specs=[spec] * count,
        compiler_params=pltpu.CompilerParams(vmem_limit_bytes=32 << 20),
        cost_estimate=pl.CostEstimate(
            flops=20 * rows * cols,
            bytes_accessed=2 * rows * cols * (len(values) + count),
            transcendentals=rows * cols,
        ),
    )(*values, *before)


def shards(
    tokens,
    cotangent,
    gate_weight,
    up_weight,
    down_weight,
    routing,
    route_weight,
    merge_source,
    merge_target,
    neuron_perm,
):
    devices_n = lax.axis_size("expert")
    hidden_n = lax.axis_size("hidden")
    me = lax.axis_index("expert")
    low_bit = lax.axis_index("hidden") % 2
    exp_local, width, neurons = gate_weight.shape
    experts = exp_local * devices_n
    tok_local, top_count = routing.shape
    tok_all = tok_local * devices_n
    depth = max(2, tok_local * top_count * 4 // (3 * experts))
    slots = devices_n * depth
    half = neurons // 2
    weights = (gate_weight, up_weight, down_weight)

    expert_ids = jnp.arange(experts, dtype=jnp.int32)
    route = jnp.sum(
        jnp.where(routing[:, :, None] == expert_ids, route_weight[:, :, None], 0.0), axis=1
    )
    high = lax.reduce_precision(route, 8, 7)
    middle = lax.reduce_precision(route - high, 8, 7)
    low = route - high - middle
    pieces = jnp.concatenate([high, middle, low], axis=1).astype(BF16)
    pad = -pieces.shape[1] % 128
    payload = jnp.concatenate([tokens, cotangent, jnp.pad(pieces, ((0, 0), (0, pad)))], axis=1)
    gathered, twins = ring_gather(payload, devices_n)

    source_dev = merge_source // exp_local
    target_dev = merge_target // exp_local
    is_source = source_dev == me
    is_target = target_dev == me
    mine = is_source | is_target
    am_target = jnp.any(is_target)
    partner = jnp.sum(jnp.where(is_source, target_dev, 0) + jnp.where(is_target, source_dev, 0))
    source_e = jnp.sum(jnp.where(mine, merge_source, 0))
    target_e = jnp.sum(jnp.where(mine, merge_target, 0))
    merged_slot = jnp.where(am_target, target_e, source_e) % exp_local
    other_slot = exp_local - 1 - merged_slot
    other_e = me * exp_local + other_slot
    perm = jnp.sum(jnp.where(mine[:, None], neuron_perm, 0), axis=0)

    order = jnp.where(am_target, jnp.arange(neurons, dtype=jnp.int32), perm)
    order = order.reshape(2, 2, half // 2)
    order = jnp.where(low_bit == 0, order, order[:, ::-1]).reshape(2, half)
    keep_order = jnp.where(am_target, order[0], order[1])
    send_order = jnp.where(am_target, order[1], order[0])
    sends, keeps = zip(*[
        slot_select(merged_slot, send_order, keep_order, w, twins[min(i, len(twins) - 1)])
        for i, w in enumerate(weights)
    ])
    others = [lax.dynamic_index_in_dim(w, other_slot, 0, keepdims=False) for w in weights]

    inputs_x = gathered[:, :width]
    inputs_c = gathered[:, width : 2 * width]
    parts = gathered[:, 2 * width : 2 * width + 3 * experts].astype(F32)
    route_all = parts[:, :experts] + parts[:, experts : 2 * experts] + parts[:, 2 * experts :]
    merged_hit = (expert_ids == source_e) | (expert_ids == target_e)
    merged_p = jnp.sum(jnp.where(merged_hit, route_all, 0.0), axis=1)
    other_p = jnp.sum(jnp.where(expert_ids == other_e, route_all, 0.0), axis=1)
    merged_dy = (merged_p[:, None] * inputs_c.astype(F32)).astype(BF16)

    named = (other_p > 0.0).reshape(devices_n, tok_local)
    upper = jnp.arange(tok_local)[:, None] <= jnp.arange(tok_local)[None, :]
    rank = dot(named.astype(BF16), upper.astype(BF16), 1, 0).astype(jnp.int32) - 1
    block = (jnp.arange(devices_n, dtype=jnp.int32) + (1 - low_bit) * (devices_n // 2)) % devices_n
    place = jnp.where(named, block[:, None] * depth + rank, -1).reshape(tok_all)
    slot_hot = jnp.arange(slots, dtype=jnp.int32)[:, None] == place[None, :]
    slot_p = jnp.sum(jnp.where(slot_hot, other_p[None, :], 0.0), axis=1)
    slot_hot = slot_hot.astype(BF16)
    other_x = dot(slot_hot, inputs_x, 1, 0).astype(BF16)
    other_dy = (dot(slot_hot, inputs_c, 1, 0) * slot_p[:, None]).astype(BF16)

    def core_sum(send_part, keep_part):
        if hidden_n == 1:
            return keep_part.astype(BF16)
        arrived = lax.ppermute(send_part.astype(BF16), "hidden", xor_pairs(hidden_n, 1))
        return (keep_part + arrived.astype(F32)).astype(BF16)

    last_bit = 2
    while last_bit * 2 < hidden_n:
        last_bit *= 2

    def near_sum(part):
        bit = 2
        while bit < last_bit:
            arrived = lax.ppermute(part, "hidden", xor_pairs(hidden_n, bit))
            part, bit = (part.astype(F32) + arrived.astype(F32)).astype(BF16), bit * 2
        return part

    def far(part):
        if last_bit < hidden_n:
            return lax.ppermute(part, "hidden", xor_pairs(hidden_n, last_bit))
        return jnp.zeros_like(part)

    def swapped(value):
        return lax.ppermute(value, "hidden", xor_pairs(hidden_n, 1))

    slots_half = slots // 2
    quarter = half // 2

    other_parts = [
        near_sum(core_sum(dot(value[:slots_half], w, 1, 0), dot(value[slots_half:], w, 1, 0)))
        for value, w in zip((other_x, other_x, other_dy), others)
    ]

    def blend(arrived, keeps, parts):
        crossed = [far(part) for part in parts]
        merged = [elementwise(mean, 1, [pair])[0] for pair in zip(keeps, arrived)]
        return merged, crossed

    merged, other_far = with_partner(devices_n, me ^ partner, sends, blend, keeps, other_parts)
    w_down = merged[2]
    merged_parts = [
        near_sum(core_sum(dot(w[quarter:], value, 1, 1), dot(w[:quarter], value, 1, 1)))
        for value, w in zip((inputs_x, inputs_x, merged_dy), merged)
    ]
    merged_sums = [(part, far(part)) for part in merged_parts[:2]]

    other_h, other_dg, other_du = [
        jnp.concatenate([swapped(a), a], axis=0)
        for a in elementwise(units_and_gradients, 3, list(zip(other_parts, other_far)))
    ]
    other_y = (dot(other_h, others[2], 1, 1) * slot_p[:, None]).astype(BF16)
    other_mixed = dot(slot_hot, other_y, 0, 0)
    other_grads, other_done = zip(*[
        slot_matmul(other_slot, value, a, exp_local)
        for value, a in ((other_x, other_dg), (other_x, other_du), (other_dy, other_h))
    ])

    def joined(a):
        return jnp.concatenate([a, swapped(a)], axis=0)

    (merged_h,) = elementwise(
        hidden_units,
        1,
        merged_sums,
        before=(other_mixed[:8, :128], merged_parts[2], *other_done),
    )
    merged_h = joined(merged_h)

    def with_back(arrived, part):
        return arrived[0], far(part)

    down_half = dot(merged_h, merged_dy, 1, 0).astype(BF16)
    far_down, back = with_partner(
        devices_n, me ^ partner, [down_half], with_back, merged_parts[2]
    )
    merged_sums.append((merged_parts[2], back))
    halves = [
        dot(joined(a), inputs_x, 1, 0).astype(BF16)
        for a in elementwise(hidden_gradients, 2, merged_sums)
    ]
    far_halves = with_partner(devices_n, me ^ partner, halves, list)

    mixed = other_mixed + merged_p[:, None] * dot(merged_h, w_down, 0, 0) + never(far_down)
    mixed = ring_scatter(mixed.astype(BF16), devices_n, far_halves[0])
    halves.append(down_half)
    far_halves.append(far_down)

    keep_flag = am_target.astype(jnp.int32)
    outs = [
        slot_place(
            merged_slot,
            keep_flag,
            low_bit,
            own,
            far,
            into,
        )
        for into, own, far in zip(
            other_grads, halves, far_halves
        )
    ]
    return (mixed, *outs)


def solution(mesh):
    placed = (
        P("expert", "hidden"),
        P("expert", "hidden"),
        P("expert", "hidden", None),
        P("expert", "hidden", None),
        P("expert", "hidden", None),
        P("expert", None),
        P("expert", None),
        P(),
        P(),
        P(),
    )
    return jax.shard_map(
        shards,
        mesh=mesh,
        in_specs=placed,
        out_specs=(
            P("expert", "hidden"),
            P("expert", "hidden", None),
            P("expert", "hidden", None),
            P("expert", "hidden", None),
        ),
        check_vma=False,
    )
```
